256 devices in a mesh: span: 4 (over y), blk: 16 (over z, x_lo), head: 4 (over x_hi, core).
Axes of the slice: x: 4 (x_hi: 2, x_lo: 2; x = x_hi * 2 + x_lo), y: 4, z: 8, core: 2. Of those that a mesh axis runs over, the one named last changes fastest.
Arguments:
- queries: bfloat16 [4, 1536, 4096], P('span', ('blk', 'head')), may hold values from -8 to 8
- keys: bfloat16 [4, 1536, 4096], P('span', ('blk', 'head')), may hold values from -8 to 8
- values: bfloat16 [4, 1536, 4096], P('span', ('blk', 'head')), may hold values from -6 to 6
- stream: bfloat16 [4, 1536, 6144], P('span', ('blk', 'head')), may hold values from -6 to 6
- latent: float32 [4, 1536, 64], P('span', ('blk', 'head')), may hold values from -6 to 6
- w_out: bfloat16 [4096, 6144], P('head'), may hold values from -0.09375 to 0.09375
- w_velocity: bfloat16 [6144, 64], replicated, may hold values from -0.078125 to 0.078125
- noise_level: int32 [4], replicated, may hold values from 0 to 7
- valid_len: int32 [4], replicated, may hold values from 768 to 1536, as said below
- span_mask: int32 [4, 4], replicated, may hold values from 0 to 1, as said below
Outputs:
- stream_out: bfloat16 [4, 1536, 6144], P('span', ('blk', 'head'))
- latent_next: float32 [4, 1536, 64], P('span', ('blk', 'head'))
The draws below stay inside these ranges and needn't reach their ends.
Inputs may be any that keep to these rules, and one draw needn't show every extreme that they name: `valid_len`: at least half of each span's tokens are valid; some span is whole in every draw. span_mask[c, c] = 1 and span_mask[c, c2] = 0 for c2 > c.
All inputs are finite; a program needn't handle non-finite values.
Results may differ from the reference program's by a relative error of at most 0.008.
Values may be sent and summed in bfloat16 or wider, within the bound.
A program may use at most 128 MiB of HBM per device.

```python
import jax
import jax.numpy as jnp
from jax import lax

D = 6144
HQ = 32
HD = 128
CH = 64
LEVELS = 8
SPANS = 4
TOK_SPAN = 1536
HGROUP = 8


def draw_queries(key, part):
    key = jax.random.fold_in(key, 11)
    field = jax.random.normal(key, (SPANS, TOK_SPAN, HQ * HD), jnp.float32)
    return jnp.clip(field, -8.0, 8.0).astype(jnp.bfloat16)


def draw_keys(key, part):
    key = jax.random.fold_in(key, 12)
    field = jax.random.normal(key, (SPANS, TOK_SPAN, HQ * HD), jnp.float32)
    return jnp.clip(field, -8.0, 8.0).astype(jnp.bfloat16)


def draw_valid_len(key, part):
    key = jax.random.fold_in(key, 13)
    first, second = jax.random.split(key)
    cuts = jax.random.randint(first, (SPANS,), 0, TOK_SPAN // 2 + 1)
    whole = jax.random.randint(second, (), 0, SPANS)
    lengths = jnp.where(jnp.arange(SPANS) == whole, TOK_SPAN, TOK_SPAN - cuts)
    return lengths.astype(jnp.int32)


def draw_span_mask(key, part):
    key = jax.random.fold_in(key, 14)
    bits = jax.random.randint(key, (SPANS, SPANS), 0, 2)
    rows = jnp.arange(SPANS)[:, None]
    cols = jnp.arange(SPANS)[None, :]
    table = jnp.where(cols < rows, bits, 0)
    table = jnp.where(cols == rows, 1, table)
    return table.astype(jnp.int32)


def with_ends(array, key, low, high):
    dims = array.shape
    place = [jax.random.randint(jax.random.fold_in(key, axis), (), 0, dims[axis]) for axis in range(len(dims))]
    array = array.at[tuple(place)].set(low)
    longest = dims.index(max(dims))
    place[longest] = (place[longest] + 1) % dims[longest]
    return array.at[tuple(place)].set(high)


def block_levels(stream_key, dims, cuts, low, high):
    gain = 1.0
    for dim, blocks in cuts:
        steps = jax.random.uniform(jax.random.fold_in(jax.random.fold_in(stream_key, 6), dim), (blocks,), jnp.float32, low / len(cuts), high / len(cuts))
        gain = gain * jnp.repeat(jnp.exp(steps), dims[dim] // blocks).reshape((-1,) + (1,) * (len(dims) - 1 - dim))
    return gain


def scatter_about(stream_key, dims, spread, limit, cuts=(), kind=jnp.bfloat16):
    array = spread * jax.random.normal(stream_key, dims, jnp.float32)
    if cuts:
        array = array * block_levels(stream_key, dims, cuts, -0.22, 0.18)
    return jnp.clip(array, -limit, limit).astype(kind)


def setup_inputs(seed: int = 0) -> dict:
    seeds = jax.random.split(jax.random.key(seed), 11)
    queries = draw_queries(jax.random.fold_in(seeds[10], 71), 0)
    keys = draw_keys(jax.random.fold_in(seeds[10], 71), 0)
    values = scatter_about(seeds[2], (SPANS, TOK_SPAN, HQ * HD), 1.0, 6.0, ((0, 4), (1, 64)))
    stream = scatter_about(seeds[3], (SPANS, TOK_SPAN, D), 1.0, 6.0, ((0, 4), (1, 64)))
    latent = scatter_about(seeds[4], (SPANS, TOK_SPAN, CH), 1.0, 6.0, ((0, 4), (1, 64)), jnp.float32)
    w_out = scatter_about(seeds[5], (HQ * HD, D), (HQ * HD) ** -0.5, 0.09375, ((0, 4),))
    w_velocity = scatter_about(seeds[6], (D, CH), D ** -0.5, 0.078125)
    noise_level = with_ends(jax.random.randint(seeds[7], (SPANS,), 0, LEVELS), jax.random.fold_in(seeds[7], 1), 0, LEVELS - 1).astype(jnp.int32)
    valid_len = draw_valid_len(jax.random.fold_in(seeds[10], 71), 0)
    span_mask = draw_span_mask(jax.random.fold_in(seeds[10], 71), 0)
    return {"queries": queries, "keys": keys, "values": values, "stream": stream, "latent": latent, "w_out": w_out, "w_velocity": w_velocity, "noise_level": noise_level, "valid_len": valid_len, "span_mask": span_mask}


def sigma_of(level):
    u = 1.0 - level.astype(jnp.float32) / LEVELS
    return 3.0 * u / (1.0 + 2.0 * u)


def reference(queries, keys, values, stream, latent, w_out, w_velocity, noise_level, valid_len, span_mask):
    spans, length, feats = queries.shape
    scale = HD ** -0.5
    positions = jnp.arange(length, dtype=jnp.int32)
    key_ok = positions[None, :] < valid_len[:, None]
    key_flat = keys.reshape(spans * length, HQ, HD)
    val_flat = values.reshape(spans * length, HQ, HD)
    query_heads = queries.reshape(spans, length, HQ, HD)

    def one_span(which):
        allowed = ((span_mask[which][:, None] == 1) & key_ok).reshape(spans * length)
        span_q = query_heads[which]

        def one_head(head_no):
            query_mat = span_q[:, head_no, :]
            key_mat = key_flat[:, head_no, :]
            val_mat = val_flat[:, head_no, :]
            scores = jnp.dot(query_mat, key_mat.T, preferred_element_type=jnp.float32) * scale
            masked = jnp.where(allowed[None, :], scores, -1e30)
            top = jnp.max(masked, axis=1, keepdims=True)
            unnorm = jnp.where(allowed[None, :], jnp.exp(masked - top), 0.0)
            total = jnp.sum(unnorm, axis=1, keepdims=True)
            summed = jnp.dot(unnorm.astype(jnp.bfloat16), val_mat, preferred_element_type=jnp.float32)
            return summed / total

        heads_out = lax.map(one_head, jnp.arange(HQ, dtype=jnp.int32))
        return jnp.transpose(heads_out, (1, 0, 2)).reshape(length, feats).astype(jnp.bfloat16)

    attn = lax.map(one_span, jnp.arange(spans, dtype=jnp.int32))
    attn_rows = attn.reshape(spans * length, feats)
    group_feats = HGROUP * HD

    def one_group(carry, group_no):
        start = (group_no * group_feats).astype(jnp.int32)
        block = lax.dynamic_slice_in_dim(attn_rows, start, group_feats, 1)
        rows_w = lax.dynamic_slice_in_dim(w_out, start, group_feats, 0)
        partial_value = jnp.dot(block, rows_w, preferred_element_type=jnp.float32).astype(jnp.bfloat16)
        return carry + partial_value.astype(jnp.float32), None

    update, _ = lax.scan(one_group, jnp.zeros((spans * length, w_out.shape[1]), jnp.float32), jnp.arange(HQ // HGROUP, dtype=jnp.int32))
    stream_out = (stream.astype(jnp.float32) + update.reshape(spans, length, -1)).astype(jnp.bfloat16)
    velocity = jnp.dot(stream_out.reshape(spans * length, -1), w_velocity, preferred_element_type=jnp.float32)
    step = sigma_of(noise_level + 1) - sigma_of(noise_level)
    latent_next = latent + step[:, None, None] * velocity.reshape(spans, length, -1)
    return stream_out, latent_next
```

```python
import functools

import jax
import jax.numpy as jnp
from jax import lax
from jax.experimental import pallas as pl
from jax.experimental.pallas import tpu as pltpu
from jax.sharding import PartitionSpec as P

HD = 128
LEVELS = 8
SPANS = 4
BLKS = 16
ROWS = 24
HEADS = 32
SLOTS = 32
TOK = SLOTS * ROWS
MODEL = 6144
GROUP = 1024
CHUNKS = 6
WIDE = MODEL // CHUNKS
SCALE = HD ** -0.5
NEG = -1e30
MESH = pl.DeviceIdType.MESH
BF = jnp.bfloat16
F32 = jnp.float32


def place():
    span = lax.axis_index("span")
    blk = lax.axis_index("blk")
    head = lax.axis_index("head")
    return span, blk, lax.div(head, 2), lax.rem(head, 2)


def flip(blk):
    return blk + 1 - 2 * lax.rem(blk, 2)


def gather_kernel(
    q_ref, k_ref, v_ref, qo_ref, kv_ref, packq, packkv, a_send, a_recv, a_own,
    y_send, y_recv, c_send, c_recv,
):
    span, blk, half, core = place()
    mine = half * BLKS + blk
    sibling = {"head": half * 2 + 1 - core}
    barrier = pltpu.get_barrier_semaphore()

    def greet(i, carry):
        other = lax.rem(mine + i, HEADS)
        pl.semaphore_signal(
            barrier, inc=1, device_id={"blk": lax.rem(other, BLKS), "head": lax.div(other, BLKS) * 2 + core},
            device_id_type=MESH,
        )
        return carry

    lax.fori_loop(1, HEADS, greet, 0)
    pl.semaphore_signal(barrier, inc=1, device_id=sibling, device_id_type=MESH)
    for i in range(1, SPANS):
        pl.semaphore_signal(barrier, inc=1, device_id={"span": lax.rem(span + i, SPANS)}, device_id_type=MESH)

    for h in range(HEADS):
        cols = slice(h * HD, (h + 1) * HD)
        packkv[h, 0] = k_ref[0, :, cols]
        packkv[h, 1] = v_ref[0, :, cols]
        packq[h] = q_ref[0, :, cols]

    pl.semaphore_wait(barrier, HEADS - 1 + 1 + SPANS - 1)

    def target(i):
        other = lax.rem(mine + i, HEADS)
        there = lax.div(other, BLKS)
        cross = lax.rem(half + there, 2)
        slot = blk + cross * (1 - 2 * lax.rem(blk, 2))
        return other, {"blk": lax.rem(other, BLKS), "head": there * 2 + core}, slot, cross

    def send_kv(i, carry):
        other, device, slot, cross = target(i)
        pltpu.make_async_remote_copy(
            packkv.at[other], kv_ref.at[span, 0, slot, cross], a_send.at[0], a_recv.at[0],
            device_id=device, device_id_type=MESH,
        ).start()
        return carry

    def send_q(i, carry):
        other, device, slot, cross = target(i)
        pltpu.make_async_remote_copy(
            packq.at[other], qo_ref.at[slot, cross], a_send.at[1], a_recv.at[1],
            device_id=device, device_id_type=MESH,
        ).start()
        return carry

    lax.fori_loop(1, HEADS, send_kv, 0)
    own_kv = pltpu.make_async_copy(packkv.at[mine], kv_ref.at[span, 0, blk, 0], a_own.at[0])
    own_q = pltpu.make_async_copy(packq.at[mine], qo_ref.at[blk, 0], a_own.at[1])
    own_kv.start()
    own_q.start()
    lax.fori_loop(1, HEADS, send_q, 0)
    own_kv.wait()

    def all_kv(sem):
        pltpu.make_async_copy(packkv.at[pl.ds(0, HEADS - 1)], packkv.at[pl.ds(0, HEADS - 1)], sem).wait()

    def all_q(sem):
        pltpu.make_async_copy(packq.at[pl.ds(0, HEADS - 1)], packq.at[pl.ds(0, HEADS - 1)], sem).wait()

    all_kv(a_recv.at[0])

    def piece(c2, p, rel=0):
        return kv_ref.at[c2, rel, pl.ds(p * 8, 8)]

    def along(c2, p, to, which):
        return pltpu.make_async_remote_copy(
            piece(c2, p), piece(c2, p), y_send.at[which], y_recv.at[c2, p],
            device_id={"span": to}, device_id_type=MESH,
        )

    def beside(c2, p):
        return pltpu.make_async_remote_copy(
            piece(c2, p), piece(c2, p, 1), c_send.at[c2, p], c_recv.at[c2, p],
            device_id=sibling, device_id_type=MESH,
        )

    @pl.when(span == 0)
    def _():
        sends = [along(0, 0, 1, 0), along(0, 1, 3, 1), along(0, 1, 1, 2), along(0, 0, 3, 3)]
        for s in sends:
            s.start()
        over = [beside(0, 0), beside(0, 1)]
        for s in over:
            s.start()
        relay = along(1, 1, 3, 4)
        relay.wait_recv()
        relay.start()
        for s in sends + [relay]:
            s.wait_send()
        for s in over:
            s.wait()

    @pl.when(span == 1)
    def _():
        sends = [along(1, 1, 0, 0), along(1, 0, 2, 1), along(1, 1, 2, 2)]
        for s in sends:
            s.start()
        over = [beside(1, 0), beside(1, 1), beside(0, 0), beside(0, 1)]
        over[0].start()
        over[1].start()
        relay = along(0, 0, 2, 3)
        relay.wait_recv()
        relay.start()
        over[2].start()
        along(0, 1, 2, 4).wait_recv()
        over[3].start()
        for s in sends + [relay]:
            s.wait_send()
        for s in over:
            s.wait()

    @pl.when(span == 2)
    def _():
        sends = [along(2, 0, 3, 0), along(2, 1, 3, 1)]
        for s in sends:
            s.start()
        over = [beside(2, 0), beside(2, 1)]
        for s in over:
            s.start()
        relay = along(1, 0, 3, 2)
        relay.wait_recv()
        relay.start()
        for c2, p in ((1, 0), (1, 1), (0, 0), (0, 1)):
            if (c2, p) != (1, 0):
                along(c2, p, 3, 3).wait_recv()
            s = beside(c2, p)
            s.start()
            over.append(s)
        for s in sends + [relay]:
            s.wait_send()
        for s in over:
            s.wait()

    @pl.when(span == 3)
    def _():
        over = [beside(3, 0), beside(3, 1)]
        for s in over:
            s.start()
        relay = along(0, 1, 2, 0)
        relay.wait_recv()
        relay.start()
        for c2, p in ((0, 1), (2, 0), (0, 0), (2, 1), (1, 0), (1, 1)):
            if (c2, p) != (0, 1):
                along(c2, p, 2, 1).wait_recv()
            s = beside(c2, p)
            s.start()
            over.append(s)
        relay.wait_send()
        for s in over:
            s.wait()

    all_q(a_recv.at[1])
    all_kv(a_send.at[0])
    all_q(a_send.at[1])
    own_q.wait()


def gather(queries, keys, values):
    vm = pl.BlockSpec(memory_space=pltpu.VMEM)
    return pl.pallas_call(
        gather_kernel,
        out_shape=(
            jax.ShapeDtypeStruct((BLKS, 2, ROWS, HD), BF),
            jax.ShapeDtypeStruct((SPANS, 2, BLKS, 2, 2, ROWS, HD), BF),
        ),
        in_specs=[vm] * 3,
        out_specs=(vm, vm),
        scratch_shapes=[
            pltpu.VMEM((HEADS, ROWS, HD), BF),
            pltpu.VMEM((HEADS, 2, ROWS, HD), BF),
            pltpu.SemaphoreType.DMA((2,)),
            pltpu.SemaphoreType.DMA((2,)),
            pltpu.SemaphoreType.DMA((2,)),
            pltpu.SemaphoreType.DMA((5,)),
            pltpu.SemaphoreType.DMA((4, 2)),
            pltpu.SemaphoreType.DMA((4, 2)),
            pltpu.SemaphoreType.DMA((4, 2)),
        ],
        compiler_params=pltpu.CompilerParams(
            collective_id=0, has_side_effects=True, vmem_limit_bytes=32 * 2**20
        ),
        name="gather",
    )(queries, keys, values)


def attend_kernel(mask_ref, valid_ref, q_ref, kv_ref, o_ref, qx, kx, vx, acc, best):
    span, blk, half, core = place()
    lane = lax.broadcasted_iota(jnp.int32, (TOK, HD), 1)
    first = lane == 0
    qx[:, :HD] = q_ref[...].reshape(TOK, HD)
    qx[:, HD:] = jnp.where(first, 1.0, 0.0).astype(BF)
    acc[...] = jnp.zeros_like(acc)
    best[...] = jnp.full_like(best, NEG)
    row = lax.broadcasted_iota(jnp.int32, (TOK, HD), 0)
    slot = lax.div(row, 2 * ROWS)
    inner = lax.rem(row, 2 * ROWS)
    cross = (inner >= ROWS).astype(jnp.int32)
    sblk = slot + cross * (1 - 2 * lax.rem(slot, 2))
    shalf = lax.rem(half + cross, 2)
    base = sblk * (4 * ROWS) + shalf * (2 * ROWS) + lax.rem(row, ROWS)
    for rel in range(2):
        vx[rel, :, HD:] = jnp.where(first, 1.0, 0.0).astype(BF)

    def one_span(c2, carry):
        @pl.when(mask_ref[span, c2] == 1)
        def _():
            for rel in range(2):
                kx[rel, :, :HD] = kv_ref[c2, rel, :, :, 0].reshape(TOK, HD)
                vx[rel, :, :HD] = kv_ref[c2, rel, :, :, 1].reshape(TOK, HD)
                pos = base + lax.rem(core + rel, 2) * ROWS
                kx[rel, :, HD:] = jnp.where(first & (pos >= valid_ref[c2]), NEG, 0.0).astype(BF)

            def tile(t, carry):
                rows = pl.ds(pl.multiple_of(t * 256, 256), 256)
                for rel in range(2):
                    scores = lax.dot_general(
                        qx[rows], kx[rel], (((1,), (1,)), ((), ())), preferred_element_type=F32
                    ) * SCALE
                    old = best[rows]
                    fresh = jnp.maximum(old, jnp.max(scores, axis=1, keepdims=True))
                    unnorm = jnp.exp(scores - fresh[:, :1]).astype(BF)
                    part = jnp.dot(unnorm, vx[rel], preferred_element_type=F32)
                    acc[rows] = acc[rows] * jnp.exp(old - fresh)[:, :1] + part
                    best[rows] = fresh
                return carry

            lax.fori_loop(0, TOK // 256, tile, 0)

        return carry

    lax.fori_loop(0, span + 1, one_span, 0)
    o_ref[...] = (acc[:, :HD] / acc[:, HD : HD + 1]).astype(BF).reshape(BLKS, 2, ROWS, HD)


def attention(span_mask, valid_len, q, kv):
    vm = pl.BlockSpec(memory_space=pltpu.VMEM)
    sm = pl.BlockSpec(memory_space=pltpu.SMEM)
    return pl.pallas_call(
        attend_kernel,
        out_shape=jax.ShapeDtypeStruct((BLKS, 2, ROWS, HD), BF),
        in_specs=[sm, sm, vm, vm],
        out_specs=vm,
        scratch_shapes=[
            pltpu.VMEM((TOK, 2 * HD), BF),
            pltpu.VMEM((2, TOK, 2 * HD), BF),
            pltpu.VMEM((2, TOK, 2 * HD), BF),
            pltpu.VMEM((TOK, 2 * HD), F32),
            pltpu.VMEM((TOK, HD), F32),
        ],
        compiler_params=pltpu.CompilerParams(vmem_limit_bytes=40 * 2**20),
        name="attend",
    )(span_mask, valid_len, q, kv)


def project_kernel(
    noise_ref, o_ref, stream_ref, latent_ref, wv_ref, w_hbm, out_ref, next_ref,
    w_buf, heads, lhs, near_out, near_in, far_out, far_in,
    w_sem, h_send, h_recv, h_own, n_send, n_recv, f_send, f_recv,
):
    span, blk, half, core = place()
    loads = [
        pltpu.make_async_copy(w_hbm.at[:, pl.ds(n * WIDE, WIDE)], w_buf.at[n], w_sem.at[n]) for n in range(CHUNKS)
    ]
    for load in loads:
        load.start()
    sibling = {"head": half * 2 + 1 - core}
    partner = {"blk": flip(blk), "head": (1 - half) * 2 + core}
    barrier = pltpu.get_barrier_semaphore()
    me = blk * 2 + core

    def greet(i, carry):
        other = lax.rem(me + i, 2 * BLKS)
        pl.semaphore_signal(
            barrier, inc=1, device_id={"blk": lax.div(other, 2), "head": half * 2 + lax.rem(other, 2)},
            device_id_type=MESH,
        )
        return carry

    lax.fori_loop(1, 2 * BLKS, greet, 0)
    pl.semaphore_signal(barrier, inc=1, device_id=partner, device_id_type=MESH)
    pl.semaphore_wait(barrier, 2 * BLKS)

    goal = lax.div(blk, 8)
    rel = lax.rem(goal + core, 2)
    lane = lax.rem(blk, 8)

    def send(i, carry):
        other = lax.rem(blk + i, BLKS)
        pltpu.make_async_remote_copy(
            o_ref.at[other], heads.at[rel, lane], h_send, h_recv,
            device_id={"blk": other, "head": half * 2 + goal}, device_id_type=MESH,
        ).start()
        return carry

    lax.fori_loop(1, BLKS, send, 0)
    keep = goal == core

    @pl.when(keep)
    def _():
        own = pltpu.make_async_copy(o_ref.at[blk], heads.at[rel, lane], h_own)
        own.start()
        own.wait()
        pltpu.make_async_copy(o_ref.at[pl.ds(0, 15)], o_ref.at[pl.ds(0, 15)], h_recv).wait()
        pltpu.make_async_copy(o_ref.at[pl.ds(0, 15)], o_ref.at[pl.ds(0, 15)], h_send).wait()

    @pl.when(jnp.logical_not(keep))
    def _():
        pltpu.make_async_remote_copy(
            o_ref.at[blk], heads.at[rel, lane], h_send, h_recv,
            device_id={"blk": blk, "head": half * 2 + goal}, device_id_type=MESH,
        ).start()
        pltpu.make_async_copy(o_ref, o_ref, h_recv).wait()
        pltpu.make_async_copy(o_ref, o_ref, h_send).wait()

    @pl.when(True)
    def _():
        for r in range(2):
            for j in range(8):
                lhs[r * 48 : (r + 1) * 48, j * HD : (j + 1) * HD] = heads[r, j].reshape(48, HD)

    def near(n):
        return pltpu.make_async_remote_copy(
            near_out.at[n], near_in.at[n], n_send.at[n], n_recv.at[n], device_id=sibling, device_id_type=MESH
        )

    def far(n):
        return pltpu.make_async_remote_copy(
            far_out.at[n], far_in.at[n], f_send.at[n], f_recv.at[n], device_id=partner, device_id_type=MESH
        )

    held = [None] * CHUNKS
    velocity = jnp.zeros((ROWS, 64), F32)
    for n in range(CHUNKS + 2):
        if n < CHUNKS:
            loads[n].wait()
            part = jnp.dot(lhs[...], w_buf[n], preferred_element_type=F32)
            near_out[n] = part[48:].astype(BF).reshape(2, ROWS, WIDE)
            near(n).start()
            held[n] = part[:48]
        m = n - 1
        if 0 <= m < CHUNKS:
            near(m).wait_recv()
            held[m] = held[m].reshape(2, ROWS, WIDE) + near_in[m].astype(F32)
            far_out[m] = held[m][1].astype(BF)
            far(m).start()
            held[m] = held[m][0]
        m = n - 2
        if 0 <= m < CHUNKS:
            far(m).wait_recv()
            cols = slice(m * WIDE, (m + 1) * WIDE)
            fresh = (stream_ref[0, :, cols].astype(F32) + (held[m] + far_in[m].astype(F32))).astype(BF)
            out_ref[0, :, cols] = fresh
            velocity += lax.dot_general(
                fresh, wv_ref[:, cols], (((1,), (1,)), ((), ())), preferred_element_type=F32
            )
    level = jnp.full((ROWS, 64), noise_ref[span], jnp.int32).astype(F32)

    def sigma(value):
        u = 1.0 - value / LEVELS
        return 3.0 * u / (1.0 + 2.0 * u)

    next_ref[0] = latent_ref[0] + (sigma(level + 1.0) - sigma(level)) * velocity
    for n in range(CHUNKS):
        near(n).wait_send()
        far(n).wait_send()


def project(noise_level, o, stream, latent, w_velocity, w_out):
    vm = pl.BlockSpec(memory_space=pltpu.VMEM)
    sm = pl.BlockSpec(memory_space=pltpu.SMEM)
    return pl.pallas_call(
        project_kernel,
        out_shape=(
            jax.ShapeDtypeStruct((1, ROWS, MODEL), BF),
            jax.ShapeDtypeStruct((1, ROWS, 64), F32),
        ),
        in_specs=[sm, vm, vm, vm, vm, pl.BlockSpec(memory_space=pl.ANY)],
        out_specs=(vm, vm),
        scratch_shapes=[
            pltpu.VMEM((CHUNKS, GROUP, WIDE), BF),
            pltpu.VMEM((2, 8, 2, ROWS, HD), BF),
            pltpu.VMEM((96, GROUP), BF),
            pltpu.VMEM((CHUNKS, 2, ROWS, WIDE), BF),
            pltpu.VMEM((CHUNKS, 2, ROWS, WIDE), BF),
            pltpu.VMEM((CHUNKS, ROWS, WIDE), BF),
            pltpu.VMEM((CHUNKS, ROWS, WIDE), BF),
            pltpu.SemaphoreType.DMA((CHUNKS,)),
            pltpu.SemaphoreType.DMA,
            pltpu.SemaphoreType.DMA,
            pltpu.SemaphoreType.DMA,
            pltpu.SemaphoreType.DMA((CHUNKS,)),
            pltpu.SemaphoreType.DMA((CHUNKS,)),
            pltpu.SemaphoreType.DMA((CHUNKS,)),
            pltpu.SemaphoreType.DMA((CHUNKS,)),
        ],
        compiler_params=pltpu.CompilerParams(
            collective_id=1, has_side_effects=True, vmem_limit_bytes=48 * 2**20
        ),
        name="project",
    )(noise_level, o, stream, latent, w_velocity.T, w_out)


def on_device(
    queries, keys, values, stream, latent, w_out, w_velocity, noise_level, valid_len, span_mask
):
    q, kv = gather(queries, keys, values)
    o = attention(span_mask, valid_len, q, kv)
    return project(noise_level, o, stream, latent, w_velocity, w_out)


def solution(mesh):
    rows = P("span", ("blk", "head"), None)
    return jax.shard_map(
        on_device,
        mesh=mesh,
        in_specs=(rows, rows, rows, rows, rows, P("head", None), P(), P(), P(), P()),
        out_specs=(rows, rows),
        check_vma=False,
    )
```

```python
import jax
import jax.numpy as jnp
from jax import lax
from jax.experimental import pallas as pl
from jax.experimental.pallas import tpu as pltpu
from jax.sharding import PartitionSpec as P

HD = 128
LEVELS = 8
SPANS = 4
BLKS = 16
ROWS = 24
HEADS = 32
SLOTS = 32
TOK = SLOTS * ROWS
MODEL = 6144
GROUP = 1024
CHUNKS = 6
WIDE = MODEL // CHUNKS
LOG_SCALE = HD ** -0.5 * 1.4426950408889634
TILE = 256
DEPTHS = (4, 0, 3, 7, 5, 1, 2, 6)
NEG = -1e30
MESH = pl.DeviceIdType.MESH
BF = jnp.bfloat16
F32 = jnp.float32


def place():
    span = lax.axis_index("span")
    blk = lax.axis_index("blk")
    head = lax.axis_index("head")
    return span, blk, lax.div(head, 2), lax.rem(head, 2)


def flip(blk):
    return blk + 1 - 2 * lax.rem(blk, 2)


def block_kernel(
    noise_ref, valid_ref, mask_ref, q_hbm, k_hbm, v_hbm, stream_hbm, latent_hbm, wv_hbm, w_hbm, out_ref, next_ref,
    q_in, k_in, v_in, stream_in, latent_in, wv_in, w_buf, q_got, kv_got, qx, kx, vx, acc, best, base, o_flat, o_buf,
    heads, lhs, near_out, near_in, far_out, far_in,
    in_sem, w_sem, a_send, a_recv, a_own, y_send, y_recv, c_send, c_recv, h_send, h_recv, h_own,
    n_send, n_recv, f_send, f_recv,
):
    span, blk, half, core = place()
    mine = half * BLKS + blk
    depth = lax.div(blk, 2)
    column = half * 2 + lax.rem(blk, 2)
    sibling = {"head": half * 2 + 1 - core}
    partner = {"blk": flip(blk), "head": (1 - half) * 2 + core}
    barrier = pltpu.get_barrier_semaphore()

    def greet(i, carry):
        other = lax.rem(mine + i, HEADS)
        pl.semaphore_signal(
            barrier, inc=1, device_id={"blk": lax.rem(other, BLKS), "head": lax.div(other, BLKS) * 2 + core},
            device_id_type=MESH,
        )
        return carry

    def greet_other(i, carry):
        pl.semaphore_signal(
            barrier, inc=1, device_id={"blk": lax.rem(blk + i, BLKS), "head": half * 2 + 1 - core}, device_id_type=MESH
        )
        return carry

    lax.fori_loop(1, HEADS, greet, 0)
    lax.fori_loop(0, BLKS, greet_other, 0)
    for i in range(1, SPANS):
        pl.semaphore_signal(barrier, inc=1, device_id={"span": lax.rem(span + i, SPANS)}, device_id_type=MESH)

    fetch = [
        pltpu.make_async_copy(src, dst, in_sem.at[i])
        for i, (src, dst) in enumerate(
            ((k_hbm, k_in), (v_hbm, v_in), (q_hbm, q_in), (stream_hbm, stream_in), (latent_hbm, latent_in), (wv_hbm, wv_in))
        )
    ]
    for copy in fetch:
        copy.start()
    loads = [
        pltpu.make_async_copy(w_hbm.at[:, pl.ds(n * WIDE, WIDE)], w_buf.at[n], w_sem.at[n]) for n in range(CHUNKS)
    ]
    lane = lax.broadcasted_iota(jnp.int32, (TOK, HD), 1)
    first = lane == 0
    row = lax.broadcasted_iota(jnp.int32, (TOK, HD), 0)
    turn = lax.div(row, ROWS)
    dz = jnp.zeros_like(turn)
    for step in range(8):
        dz = jnp.where(lax.div(turn, 4) == step, DEPTHS[step], dz)
    z = lax.rem(depth + 8 - dz, 8)
    x = lax.rem(column + 4 - lax.rem(turn, 4), 4)
    base[...] = (z * 2 + lax.rem(x, 2)) * (4 * ROWS) + lax.div(x, 2) * (2 * ROWS) + lax.rem(row, ROWS)
    unit = jnp.where(first, 1.0, 0.0).astype(BF)
    qx[:, HD:] = unit
    acc[...] = jnp.zeros_like(acc)
    best[...] = jnp.full_like(best, NEG)

    def prepare(c2, carry):
        limit = valid_ref[c2] * mask_ref[span, c2]
        for rel in range(2):
            here = pl.ds(rel * TOK, TOK)
            vx[c2, here, HD:] = unit
            pos = base[...] + lax.rem(core + rel, 2) * ROWS
            kx[c2, here, HD:] = jnp.where(first & (pos >= limit), NEG, 0.0).astype(BF)
        return carry

    lax.fori_loop(0, span + 1, prepare, 0)
    for i in range(3):
        fetch[i].wait()
    pl.semaphore_wait(barrier, HEADS - 1 + BLKS + SPANS - 1)

    def cols(head):
        return pl.ds(pl.multiple_of(head * HD, HD), HD)

    def target(dz, dx):
        z = lax.rem(depth + dz, 8)
        x = lax.rem(column + dx, 4)
        there = lax.div(x, 2)
        to = z * 2 + lax.rem(x, 2)
        return there * BLKS + to, {"blk": to, "head": there * 2 + core}, there

    own = [
        pltpu.make_async_copy(k_in.at[0, :, cols(mine)], kv_got.at[span, 0, 0, 0, 4], a_own.at[0]),
        pltpu.make_async_copy(v_in.at[0, :, cols(mine)], kv_got.at[span, 0, 0, 1, 4], a_own.at[1]),
        pltpu.make_async_copy(q_in.at[0, :, cols(mine)], q_got.at[BLKS + blk], a_own.at[2]),
    ]
    for step, dz in enumerate(DEPTHS):
        j, s = step // 2, step % 2 * 4

        def send_kv(dx, carry, dz=dz, j=j, s=s):
            other, device, there = target(dz, dx)
            for t, src in enumerate((k_in, v_in)):
                pltpu.make_async_remote_copy(
                    src.at[0, :, cols(other)], kv_got.at[span, 0, j, t, s + dx], a_send.at[t], a_recv.at[j],
                    device_id=device, device_id_type=MESH,
                ).start()
            return carry

        lax.fori_loop(0 if dz else 1, 4, send_kv, 0)
    for copy in own:
        copy.start()
    for dz in DEPTHS:

        def send_q(dx, carry, dz=dz):
            other, device, there = target(dz, dx)
            cross = lax.rem(half + there, 2)
            slot = (1 - cross) * BLKS + blk + cross * (1 - 2 * lax.rem(blk, 2))
            pltpu.make_async_remote_copy(
                q_in.at[0, :, cols(other)], q_got.at[slot], a_send.at[2], a_recv.at[4],
                device_id=device, device_id_type=MESH,
            ).start()
            return carry

        lax.fori_loop(0 if dz else 1, 4, send_q, 0)
    for load in loads:
        load.start()
    own[0].wait()
    own[1].wait()

    def arrived(j):
        count = 8 if j else 7
        whole = kv_got.at[0, 0, 0, :, pl.ds(0, count)]
        pltpu.make_async_copy(whole, whole, a_recv.at[j]).wait()

    def along(c2, j, to, which):
        return pltpu.make_async_remote_copy(
            kv_got.at[c2, 0, j], kv_got.at[c2, 0, j], y_send.at[which], y_recv.at[c2, j],
            device_id={"span": to}, device_id_type=MESH,
        )

    def beside(c2, j):
        return pltpu.make_async_remote_copy(
            kv_got.at[c2, 0, j], kv_got.at[c2, 1, j], c_send.at[c2, j], c_recv.at[c2, j],
            device_id=sibling, device_id_type=MESH,
        )

    plans = (
        "A0>1,3;A1>1,3;A2>1,3;R11>3;A3>1,3,2",
        "A0>2;A1>0,2;R00>2;A2>2;R01;A3>2,3",
        "A0>3;A1>3;R10>3;A2>3;R00;R01;A3>3;R11;R12>3",
        "A0;A1;R01>2;A2;R20;R00;R10;R21;R02>2;A3;R11;R22",
    )
    later = ("", "R02;R03", "R02;R13;R03", "R12;R23;R03;R13")

    def play(c, plan, count=0):
        sends, over = [], []
        for event in plan.split(";") if plan else ():
            what, _, to = event.partition(">")
            if what[0] == "A":
                c2, j = c, int(what[1])
                arrived(j)
            else:
                c2, j = int(what[1]), int(what[2])
                along(c2, j, 0, 0).wait_recv()
            for t in to.split(",") if to else ():
                copy = along(c2, j, int(t), count + len(sends))
                copy.start()
                sends.append(copy)
            if c2 <= c:
                copy = beside(c2, j)
                copy.start()
                over.append(copy)
        return sends, over

    for c in range(SPANS):

        @pl.when(span == c)
        def _(c=c):
            sends, over = play(c, plans[c])
            for copy in sends:
                copy.wait_send()
            for copy in over:
                copy.wait_send()

    own[2].wait()
    others = q_got.at[pl.ds(0, HEADS - 1)]
    pltpu.make_async_copy(others, others, a_recv.at[4]).wait()
    qx[:, :HD] = q_got[...].reshape(TOK, HD)

    goal = lax.div(blk, 8)
    rel = lax.rem(goal + core, 2)
    place_in = lax.rem(blk, 8)
    keep = goal == core

    def compute(c2, finish):
        for j in range(4):
            beside(c2, j).wait_recv()
        for r in range(2):
            here = pl.ds(r * TOK, TOK)
            kx[c2, here, :HD] = kv_got[c2, r, :, 0].reshape(TOK, HD)
            vx[c2, here, :HD] = kv_got[c2, r, :, 1].reshape(TOK, HD)
        for t in range(TOK // TILE):
            rows = slice(t * TILE, (t + 1) * TILE)
            scores = lax.dot_general(
                qx[rows], kx[c2], (((1,), (1,)), ((), ())), preferred_element_type=F32
            )
            old = best[rows]
            fresh = jnp.maximum(old, jnp.max(scores, axis=1, keepdims=True))
            unnorm = jnp.exp2(scores * LOG_SCALE - (fresh * LOG_SCALE)[:, :1]).astype(BF)
            part = jnp.dot(unnorm, vx[c2], preferred_element_type=F32)
            total = acc[rows] * jnp.exp2((old - fresh) * LOG_SCALE)[:, :1] + part
            if finish:
                o_flat[rows] = (total[:, :HD] / total[:, HD : HD + 1]).astype(BF)
                if t:
                    send_part(t - 1)
            else:
                acc[rows] = total
                best[rows] = fresh

    def send_part(part):
        here = pl.ds(part * BLKS, BLKS)
        o_buf[here] = o_flat[part * BLKS * ROWS : (part + 1) * BLKS * ROWS].reshape(BLKS, ROWS, HD)

        def send_o(i, carry):
            other = lax.rem(blk + i, BLKS)
            pltpu.make_async_remote_copy(
                o_buf.at[part * BLKS + other], heads.at[part, rel, place_in], h_send.at[part], h_recv.at[part],
                device_id={"blk": other, "head": half * 2 + goal}, device_id_type=MESH,
            ).start()
            return carry

        lax.fori_loop(1, BLKS, send_o, 0)

        @pl.when(keep)
        def _():
            pltpu.make_async_copy(
                o_buf.at[part * BLKS + blk], heads.at[part, rel, place_in], h_own.at[part]
            ).start()

        @pl.when(jnp.logical_not(keep))
        def _():
            send_o(0, 0)

    def wait_part(part):
        most, every = o_buf.at[pl.ds(0, BLKS - 1)], o_buf.at[pl.ds(0, BLKS)]

        @pl.when(keep)
        def _():
            pltpu.make_async_copy(
                o_buf.at[part * BLKS + blk], heads.at[part, rel, place_in], h_own.at[part]
            ).wait()
            pltpu.make_async_copy(most, most, h_recv.at[part]).wait()
            pltpu.make_async_copy(most, most, h_send.at[part]).wait()

        @pl.when(jnp.logical_not(keep))
        def _():
            pltpu.make_async_copy(every, every, h_recv.at[part]).wait()
            pltpu.make_async_copy(every, every, h_send.at[part]).wait()

        for r in range(2):
            for j in range(8):
                lhs[part, r * ROWS : (r + 1) * ROWS, j * HD : (j + 1) * HD] = heads[part, r, j]

    def one_span(i, carry):
        compute(span - i, False)
        for c in range(1, SPANS):

            @pl.when((span == c) & (i == 0))
            def _(c=c):
                sends, over = play(c, later[c])
                for copy in over:
                    copy.wait_send()

        return carry

    lax.fori_loop(0, span, one_span, 0)
    compute(0, True)

    def near(part, n):
        return pltpu.make_async_remote_copy(
            near_out.at[part, n], near_in.at[part, n], n_send.at[part, n], n_recv.at[part, n],
            device_id=sibling, device_id_type=MESH,
        )

    def far(n):
        return pltpu.make_async_remote_copy(
            far_out.at[n], far_in.at[n], f_send.at[n], f_recv.at[n], device_id=partner, device_id_type=MESH
        )

    wait_part(0)
    held = [None] * CHUNKS
    for n in range(CHUNKS + 1):
        if n < CHUNKS:
            loads[n].wait()
            part = jnp.dot(lhs[0], w_buf[n], preferred_element_type=F32)
            near_out[0, n] = part[ROWS:].astype(BF)
            near(0, n).start()
            held[n] = part[:ROWS]
        m = n - 1
        if 0 <= m < CHUNKS:
            near(0, m).wait_recv()
            far_out[m] = (held[m] + near_in[0, m].astype(F32)).astype(BF)
            far(m).start()
    wait_part(1)
    for n in range(CHUNKS):
        part = jnp.dot(lhs[1], w_buf[n], preferred_element_type=F32)
        near_out[1, n] = part[ROWS:].astype(BF)
        near(1, n).start()
        held[n] = part[:ROWS]
    for i in range(3, 6):
        fetch[i].wait()
    velocity = jnp.zeros((ROWS, 64), F32)
    for m in range(CHUNKS):
        near(1, m).wait_recv()
        far(m).wait_recv()
        here = slice(m * WIDE, (m + 1) * WIDE)
        update = held[m] + near_in[1, m].astype(F32) + far_in[m].astype(F32)
        fresh = (stream_in[0, :, here].astype(F32) + update).astype(BF)
        out_ref[0, :, here] = fresh
        velocity += lax.dot_general(
            fresh, wv_in[:, here], (((1,), (1,)), ((), ())), preferred_element_type=F32
        )
    level = jnp.full((ROWS, 64), noise_ref[span], jnp.int32).astype(F32)

    def sigma(value):
        u = 1.0 - value / LEVELS
        return 3.0 * u / (1.0 + 2.0 * u)

    next_ref[0] = latent_in[0] + (sigma(level + 1.0) - sigma(level)) * velocity
    for t in range(3):
        pltpu.make_async_copy(others, others, a_send.at[t]).wait()
    for n in range(CHUNKS):
        near(0, n).wait_send()
        near(1, n).wait_send()
        far(n).wait_send()


def finish_kernel(rows_in, next_in, rows_out, next_out, rows_buf, next_buf, in_sem, out_sem):
    wide = MODEL // 4
    first, second = [], []
    for n in range(4):
        here = (slice(None), slice(None), pl.ds(n * wide, wide))
        first.append(pltpu.make_async_copy(rows_in.at[here], rows_buf.at[here], in_sem.at[n]))
        second.append(pltpu.make_async_copy(rows_buf.at[here], rows_out.at[here], out_sem.at[n]))
    first.append(pltpu.make_async_copy(next_in, next_buf, in_sem.at[4]))
    second.append(pltpu.make_async_copy(next_buf, next_out, out_sem.at[4]))
    for copy in first:
        copy.start()
    for one, two in zip(first, second):
        one.wait()
        two.start()
    for copy in second:
        copy.wait()


def on_device(
    queries, keys, values, stream, latent, w_out, w_velocity, noise_level, valid_len, span_mask
):
    anywhere = pl.BlockSpec(memory_space=pl.ANY)
    sm = pl.BlockSpec(memory_space=pltpu.SMEM)
    vm = pl.BlockSpec(memory_space=pltpu.VMEM)
    dma = pltpu.SemaphoreType.DMA
    rows, following = pl.pallas_call(
        block_kernel,
        out_shape=(
            jax.ShapeDtypeStruct((1, ROWS, MODEL), BF),
            jax.ShapeDtypeStruct((1, ROWS, 64), F32),
        ),
        in_specs=[sm] * 3 + [anywhere] * 7,
        out_specs=(vm, vm),
        scratch_shapes=[
            pltpu.VMEM((1, ROWS, HEADS * HD), BF),
            pltpu.VMEM((1, ROWS, HEADS * HD), BF),
            pltpu.VMEM((1, ROWS, HEADS * HD), BF),
            pltpu.VMEM((1, ROWS, MODEL), BF),
            pltpu.VMEM((1, ROWS, 64), F32),
            pltpu.VMEM((64, MODEL), BF),
            pltpu.VMEM((CHUNKS, GROUP, WIDE), BF),
            pltpu.VMEM((SLOTS, ROWS, HD), BF),
            pltpu.VMEM((SPANS, 2, 4, 2, 8, ROWS, HD), BF),
            pltpu.VMEM((TOK, 2 * HD), BF),
            pltpu.VMEM((SPANS, 2 * TOK, 2 * HD), BF),
            pltpu.VMEM((SPANS, 2 * TOK, 2 * HD), BF),
            pltpu.VMEM((TOK, 2 * HD), F32),
            pltpu.VMEM((TOK, HD), F32),
            pltpu.VMEM((TOK, HD), jnp.int32),
            pltpu.VMEM((TOK, HD), BF),
            pltpu.VMEM((SLOTS, ROWS, HD), BF),
            pltpu.VMEM((2, 2, 8, ROWS, HD), BF),
            pltpu.VMEM((2, 2 * ROWS, GROUP), BF),
            pltpu.VMEM((2, CHUNKS, ROWS, WIDE), BF),
            pltpu.VMEM((2, CHUNKS, ROWS, WIDE), BF),
            pltpu.VMEM((CHUNKS, ROWS, WIDE), BF),
            pltpu.VMEM((CHUNKS, ROWS, WIDE), BF),
            dma((6,)),
            dma((CHUNKS,)),
            dma((3,)),
            dma((5,)),
            dma((3,)),
            dma((10,)),
            dma((4, 4)),
            dma((4, 4)),
            dma((4, 4)),
            dma((2,)),
            dma((2,)),
            dma((2,)),
            dma((2, CHUNKS)),
            dma((2, CHUNKS)),
            dma((CHUNKS,)),
            dma((CHUNKS,)),
        ],
        compiler_params=pltpu.CompilerParams(
            collective_id=0, has_side_effects=True, vmem_limit_bytes=58 * 2**20
        ),
        name="block",
    )(noise_level, valid_len, span_mask, queries, keys, values, stream, latent, w_velocity.T, w_out)
    return pl.pallas_call(
        finish_kernel,
        out_shape=(
            jax.ShapeDtypeStruct((1, ROWS, MODEL), BF),
            jax.ShapeDtypeStruct((1, ROWS, 64), F32),
        ),
        in_specs=[anywhere] * 2,
        out_specs=(anywhere, anywhere),
        scratch_shapes=[
            pltpu.VMEM((1, ROWS, MODEL), BF),
            pltpu.VMEM((1, ROWS, 64), F32),
            dma((5,)),
            dma((5,)),
        ],
        compiler_params=pltpu.CompilerParams(vmem_limit_bytes=58 * 2**20),
        name="finish",
    )(rows, following)


def solution(mesh):
    rows = P("span", ("blk", "head"), None)
    return jax.shard_map(
        on_device,
        mesh=mesh,
        in_specs=(rows, rows, rows, rows, rows, P("head", None), P(), P(), P(), P()),
        out_specs=(rows, rows),
        check_vma=False,
    )
```

```python
import jax
import jax.numpy as jnp
from jax import lax
from jax.experimental import pallas as pl
from jax.experimental.pallas import tpu as pltpu
from jax.sharding import PartitionSpec as P

HD = 128
LEVELS = 8
SPANS = 4
BLKS = 16
ROWS = 24
HEADS = 32
SLOTS = 32
TOK = SLOTS * ROWS
MODEL = 6144
GROUP = 1024
CHUNKS = 6
WIDE = MODEL // CHUNKS
LOG_SCALE = HD ** -0.5 * 1.4426950408889634
TILE = 256
DEPTHS = (0, 1, 7, 2, 6, 3, 5, 4)
HOME = DEPTHS.index(0)
NEG = -1e30
MESH = pl.DeviceIdType.MESH
BF = jnp.bfloat16
F32 = jnp.float32


def place():
    span = lax.axis_index("span")
    blk = lax.axis_index("blk")
    head = lax.axis_index("head")
    return span, blk, lax.div(head, 2), lax.rem(head, 2)


def flip(blk):
    return blk + 1 - 2 * lax.rem(blk, 2)


def block_kernel(
    noise_ref, valid_ref, mask_ref, q_hbm, k_hbm, v_hbm, stream_hbm, latent_hbm, wv_hbm, w_hbm, out_ref, next_ref,
    q_in, k_in, v_in, stream_in, latent_in, wv_in, w_buf, q_got, kv_got, qx, kx, vx, acc, best, base, o_flat, o_buf,
    heads, lhs, near_out, near_in, far_out, far_in,
    in_sem, w_sem, a_send, a_recv, a_own, y_send, y_recv, c_send, c_recv, h_send, h_recv, h_own,
    n_send, n_recv, f_send, f_recv,
):
    span, blk, half, core = place()
    mine = half * BLKS + blk
    depth = lax.div(blk, 2)
    column = half * 2 + lax.rem(blk, 2)
    sibling = {"head": half * 2 + 1 - core}
    partner = {"blk": flip(blk), "head": (1 - half) * 2 + core}
    barrier = pltpu.get_barrier_semaphore()

    def greet(i, carry):
        other = lax.rem(mine + i, HEADS)
        pl.semaphore_signal(
            barrier, inc=1, device_id={"blk": lax.rem(other, BLKS), "head": lax.div(other, BLKS) * 2 + core},
            device_id_type=MESH,
        )
        return carry

    def greet_other(i, carry):
        pl.semaphore_signal(
            barrier, inc=1, device_id={"blk": lax.rem(blk + i, BLKS), "head": half * 2 + 1 - core}, device_id_type=MESH
        )
        return carry

    lax.fori_loop(1, HEADS, greet, 0)
    lax.fori_loop(0, BLKS, greet_other, 0)
    for i in range(1, SPANS):
        pl.semaphore_signal(barrier, inc=1, device_id={"span": lax.rem(span + i, SPANS)}, device_id_type=MESH)

    fetch = [
        pltpu.make_async_copy(src, dst, in_sem.at[i])
        for i, (src, dst) in enumerate(
            ((k_hbm, k_in), (v_hbm, v_in), (q_hbm, q_in), (stream_hbm, stream_in), (latent_hbm, latent_in), (wv_hbm, wv_in))
        )
    ]
    for copy in fetch:
        copy.start()
    loads = [
        pltpu.make_async_copy(w_hbm.at[:, pl.ds(n * WIDE, WIDE)], w_buf.at[n], w_sem.at[n]) for n in range(CHUNKS)
    ]
    lane = lax.broadcasted_iota(jnp.int32, (TOK, HD), 1)
    first = lane == 0
    row = lax.broadcasted_iota(jnp.int32, (TOK, HD), 0)
    turn = lax.div(row, ROWS)
    dz = jnp.zeros_like(turn)
    for step in range(8):
        dz = jnp.where(lax.div(turn, 4) == step, DEPTHS[step], dz)
    z = lax.rem(depth + 8 - dz, 8)
    x = lax.rem(column + 4 - lax.rem(turn, 4), 4)
    base[...] = (z * 2 + lax.rem(x, 2)) * (4 * ROWS) + lax.div(x, 2) * (2 * ROWS) + lax.rem(row, ROWS)
    unit = jnp.where(first, 1.0, 0.0).astype(BF)
    qx[:, HD:] = unit
    acc[...] = jnp.zeros_like(acc)
    best[...] = jnp.full_like(best, NEG)

    def prepare(c2, carry):
        limit = valid_ref[c2] * mask_ref[span, c2]
        for rel in range(2):
            here = pl.ds(rel * TOK, TOK)
            vx[c2, here, HD:] = unit
            pos = base[...] + lax.rem(core + rel, 2) * ROWS
            kx[c2, here, HD:] = jnp.where(first & (pos >= limit), NEG, 0.0).astype(BF)
        return carry

    lax.fori_loop(0, span + 1, prepare, 0)
    for i in range(3):
        fetch[i].wait()
    pl.semaphore_wait(barrier, HEADS - 1 + BLKS + SPANS - 1)

    def cols(head):
        return pl.ds(pl.multiple_of(head * HD, HD), HD)

    def target(dz, dx):
        z = lax.rem(depth + dz, 8)
        x = lax.rem(column + dx, 4)
        there = lax.div(x, 2)
        to = z * 2 + lax.rem(x, 2)
        return there * BLKS + to, {"blk": to, "head": there * 2 + core}, there

    own = [
        pltpu.make_async_copy(k_in.at[0, :, cols(mine)], kv_got.at[span, 0, HOME // 2, 0, HOME % 2 * 4], a_own.at[0]),
        pltpu.make_async_copy(v_in.at[0, :, cols(mine)], kv_got.at[span, 0, HOME // 2, 1, HOME % 2 * 4], a_own.at[1]),
        pltpu.make_async_copy(q_in.at[0, :, cols(mine)], q_got.at[BLKS + blk], a_own.at[2]),
    ]
    for step, dz in enumerate(DEPTHS):
        j, s = step // 2, step % 2 * 4

        def send_kv(dx, carry, dz=dz, j=j, s=s):
            other, device, there = target(dz, dx)
            for t, src in enumerate((k_in, v_in)):
                pltpu.make_async_remote_copy(
                    src.at[0, :, cols(other)], kv_got.at[span, 0, j, t, s + dx], a_send.at[t], a_recv.at[j],
                    device_id=device, device_id_type=MESH,
                ).start()
            return carry

        lax.fori_loop(0 if dz else 1, 4, send_kv, 0)
    for copy in own:
        copy.start()
    for dz in DEPTHS:

        def send_q(dx, carry, dz=dz):
            other, device, there = target(dz, dx)
            cross = lax.rem(half + there, 2)
            slot = (1 - cross) * BLKS + blk + cross * (1 - 2 * lax.rem(blk, 2))
            pltpu.make_async_remote_copy(
                q_in.at[0, :, cols(other)], q_got.at[slot], a_send.at[2], a_recv.at[4],
                device_id=device, device_id_type=MESH,
            ).start()
            return carry

        lax.fori_loop(0 if dz else 1, 4, send_q, 0)
    for load in loads:
        load.start()
    own[0].wait()
    own[1].wait()

    def arrived(j):
        count = 7 if j == HOME // 2 else 8
        whole = kv_got.at[0, 0, 0, :, pl.ds(0, count)]
        pltpu.make_async_copy(whole, whole, a_recv.at[j]).wait()

    def along(c2, j, to, which):
        return pltpu.make_async_remote_copy(
            kv_got.at[c2, 0, j], kv_got.at[c2, 0, j], y_send.at[which], y_recv.at[c2, j],
            device_id={"span": to}, device_id_type=MESH,
        )

    def beside(c2, j):
        return pltpu.make_async_remote_copy(
            kv_got.at[c2, 0, j], kv_got.at[c2, 1, j], c_send.at[c2, j], c_recv.at[c2, j],
            device_id=sibling, device_id_type=MESH,
        )

    plans = (
        "A0>1,3;A1>1,3;R11>3;A2>1,3,2;A3>1,3,2",
        "A0>2;A1>0,2;R00>2;A2>2,3;A3>2,3",
        "A0>3;A1>3;R10>3;A2>3;R00;A3>3",
        "A0;A1;R01>2;A2;R20;R00;R10;A3",
    )
    later = (("", ""), ("R01;R02;R03", ""), ("R11;R12;R13;R01", "R02;R03"), ("R21;R22;R23;R11", "R02;R03;R12;R13"))
    started = [([], []) for _ in range(SPANS)]

    def play(c, plan):
        sends, over = started[c]
        for event in plan.split(";") if plan else ():
            what, _, to = event.partition(">")
            if what[0] == "A":
                c2, j = c, int(what[1])
                arrived(j)
            else:
                c2, j = int(what[1]), int(what[2])
                along(c2, j, 0, 0).wait_recv()
            for t in to.split(",") if to else ():
                sends.append((c2, j, int(t), len(sends)))
                along(*sends[-1]).start()
            if c2 <= c:
                over.append((c2, j))
                beside(c2, j).start()

    def settle():
        for c in range(SPANS):

            @pl.when(span == c)
            def _(c=c):
                sends, over = started[c]
                for what in sends:
                    along(*what).wait_send()
                for what in over:
                    beside(*what).wait_send()


    for c in range(SPANS):

        @pl.when(span == c)
        def _(c=c):
            play(c, plans[c])

    own[2].wait()
    others = q_got.at[pl.ds(0, HEADS - 1)]
    pltpu.make_async_copy(others, others, a_recv.at[4]).wait()
    qx[:, :HD] = q_got[...].reshape(TOK, HD)

    goal = lax.div(blk, 8)
    rel = lax.rem(goal + core, 2)
    place_in = lax.rem(blk, 8)
    keep = goal == core

    def compute(c2, finish):
        for j in range(4):
            beside(c2, j).wait_recv()
        for r in range(2):
            here = pl.ds(r * TOK, TOK)
            kx[c2, here, :HD] = kv_got[c2, r, :, 0].reshape(TOK, HD)
            vx[c2, here, :HD] = kv_got[c2, r, :, 1].reshape(TOK, HD)
        for t in range(TOK // TILE):
            rows = slice(t * TILE, (t + 1) * TILE)
            scores = lax.dot_general(
                qx[rows], kx[c2], (((1,), (1,)), ((), ())), preferred_element_type=F32
            )
            old = best[rows]
            fresh = jnp.maximum(old, jnp.max(scores, axis=1, keepdims=True))
            unnorm = jnp.exp2(scores * LOG_SCALE - (fresh * LOG_SCALE)[:, :1]).astype(BF)
            part = jnp.dot(unnorm, vx[c2], preferred_element_type=F32)
            total = acc[rows] * jnp.exp2((old - fresh) * LOG_SCALE)[:, :1] + part
            if finish:
                o_flat[rows] = (total[:, :HD] / total[:, HD : HD + 1]).astype(BF)
                if t:
                    send_part(t - 1)
            else:
                acc[rows] = total
                best[rows] = fresh

    def send_part(part):
        here = pl.ds(part * BLKS, BLKS)
        o_buf[here] = o_flat[part * BLKS * ROWS : (part + 1) * BLKS * ROWS].reshape(BLKS, ROWS, HD)

        def send_o(other):
            pltpu.make_async_remote_copy(
                o_buf.at[part * BLKS + other], heads.at[part, rel, place_in], h_send.at[part], h_recv.at[part],
                device_id={"blk": other, "head": half * 2 + goal}, device_id_type=MESH,
            ).start()

        for dz in DEPTHS:
            for dx in range(2):
                if dz or dx:
                    send_o(lax.rem(depth + dz, 8) * 2 + lax.rem(blk + dx, 2))

        @pl.when(keep)
        def _():
            pltpu.make_async_copy(
                o_buf.at[part * BLKS + blk], heads.at[part, rel, place_in], h_own.at[part]
            ).start()

        @pl.when(jnp.logical_not(keep))
        def _():
            send_o(blk)

    def wait_part(part):
        most, every = o_buf.at[pl.ds(0, BLKS - 1)], o_buf.at[pl.ds(0, BLKS)]

        @pl.when(keep)
        def _():
            pltpu.make_async_copy(
                o_buf.at[part * BLKS + blk], heads.at[part, rel, place_in], h_own.at[part]
            ).wait()
            pltpu.make_async_copy(most, most, h_recv.at[part]).wait()
            pltpu.make_async_copy(most, most, h_send.at[part]).wait()

        @pl.when(jnp.logical_not(keep))
        def _():
            pltpu.make_async_copy(every, every, h_recv.at[part]).wait()
            pltpu.make_async_copy(every, every, h_send.at[part]).wait()

        for r in range(2):
            for j in range(8):
                lhs[part, r * ROWS : (r + 1) * ROWS, j * HD : (j + 1) * HD] = heads[part, r, j]

    def one_span(i, carry):
        compute(span - i, False)
        for c in range(1, SPANS):
            for turn, plan in enumerate(later[c]):
                if plan:

                    @pl.when((span == c) & (i == turn))
                    def _(c=c, plan=plan):
                        play(c, plan)

        return carry

    lax.fori_loop(0, span, one_span, 0)
    compute(0, True)

    def near(part, n):
        return pltpu.make_async_remote_copy(
            near_out.at[part, n], near_in.at[part, n], n_send.at[part, n], n_recv.at[part, n],
            device_id=sibling, device_id_type=MESH,
        )

    def far(n):
        return pltpu.make_async_remote_copy(
            far_out.at[n], far_in.at[n], f_send.at[n], f_recv.at[n], device_id=partner, device_id_type=MESH
        )

    wait_part(0)
    held = [None] * CHUNKS
    for n in range(CHUNKS + 1):
        if n < CHUNKS:
            loads[n].wait()
            part = jnp.dot(lhs[0], w_buf[n], preferred_element_type=F32)
            near_out[0, n] = part[ROWS:].astype(BF)
            near(0, n).start()
            held[n] = part[:ROWS]
        m = n - 1
        if 0 <= m < CHUNKS:
            near(0, m).wait_recv()
            far_out[m] = (held[m] + near_in[0, m].astype(F32)).astype(BF)
            far(m).start()
    wait_part(1)
    for n in range(CHUNKS):
        part = jnp.dot(lhs[1], w_buf[n], preferred_element_type=F32)
        near_out[1, n] = part[ROWS:].astype(BF)
        near(1, n).start()
        held[n] = part[:ROWS]
    for i in range(3, 6):
        fetch[i].wait()
    velocity = jnp.zeros((ROWS, 64), F32)
    for m in range(CHUNKS):
        near(1, m).wait_recv()
        far(m).wait_recv()
        here = slice(m * WIDE, (m + 1) * WIDE)
        update = held[m] + near_in[1, m].astype(F32) + far_in[m].astype(F32)
        fresh = (stream_in[0, :, here].astype(F32) + update).astype(BF)
        out_ref[0, :, here] = fresh
        velocity += lax.dot_general(
            fresh, wv_in[:, here], (((1,), (1,)), ((), ())), preferred_element_type=F32
        )
    level = jnp.full((ROWS, 64), noise_ref[span], jnp.int32).astype(F32)

    def sigma(value):
        u = 1.0 - value / LEVELS
        return 3.0 * u / (1.0 + 2.0 * u)

    next_ref[0] = latent_in[0] + (sigma(level + 1.0) - sigma(level)) * velocity
    settle()
    for t in range(3):
        pltpu.make_async_copy(others, others, a_send.at[t]).wait()
    for n in range(CHUNKS):
        near(0, n).wait_send()
        near(1, n).wait_send()
        far(n).wait_send()


def finish_kernel(rows_in, next_in, rows_out, next_out, rows_buf, next_buf, in_sem, out_sem):
    wide = MODEL // 4
    first, second = [], []
    for n in range(4):
        here = (slice(None), slice(None), pl.ds(n * wide, wide))
        first.append(pltpu.make_async_copy(rows_in.at[here], rows_buf.at[here], in_sem.at[n]))
        second.append(pltpu.make_async_copy(rows_buf.at[here], rows_out.at[here], out_sem.at[n]))
    first.append(pltpu.make_async_copy(next_in, next_buf, in_sem.at[4]))
    second.append(pltpu.make_async_copy(next_buf, next_out, out_sem.at[4]))
    for copy in first:
        copy.start()
    for one, two in zip(first, second):
        one.wait()
        two.start()
    for copy in second:
        copy.wait()


def on_device(
    queries, keys, values, stream, latent, w_out, w_velocity, noise_level, valid_len, span_mask
):
    anywhere = pl.BlockSpec(memory_space=pl.ANY)
    sm = pl.BlockSpec(memory_space=pltpu.SMEM)
    vm = pl.BlockSpec(memory_space=pltpu.VMEM)
    dma = pltpu.SemaphoreType.DMA
    rows, following = pl.pallas_call(
        block_kernel,
        out_shape=(
            jax.ShapeDtypeStruct((1, ROWS, MODEL), BF),
            jax.ShapeDtypeStruct((1, ROWS, 64), F32),
        ),
        in_specs=[sm] * 3 + [anywhere] * 7,
        out_specs=(vm, vm),
        scratch_shapes=[
            pltpu.VMEM((1, ROWS, HEADS * HD), BF),
            pltpu.VMEM((1, ROWS, HEADS * HD), BF),
            pltpu.VMEM((1, ROWS, HEADS * HD), BF),
            pltpu.VMEM((1, ROWS, MODEL), BF),
            pltpu.VMEM((1, ROWS, 64), F32),
            pltpu.VMEM((64, MODEL), BF),
            pltpu.VMEM((CHUNKS, GROUP, WIDE), BF),
            pltpu.VMEM((SLOTS, ROWS, HD), BF),
            pltpu.VMEM((SPANS, 2, 4, 2, 8, ROWS, HD), BF),
            pltpu.VMEM((TOK, 2 * HD), BF),
            pltpu.VMEM((SPANS, 2 * TOK, 2 * HD), BF),
            pltpu.VMEM((SPANS, 2 * TOK, 2 * HD), BF),
            pltpu.VMEM((TOK, 2 * HD), F32),
            pltpu.VMEM((TOK, HD), F32),
            pltpu.VMEM((TOK, HD), jnp.int32),
            pltpu.VMEM((TOK, HD), BF),
            pltpu.VMEM((SLOTS, ROWS, HD), BF),
            pltpu.VMEM((2, 2, 8, ROWS, HD), BF),
            pltpu.VMEM((2, 2 * ROWS, GROUP), BF),
            pltpu.VMEM((2, CHUNKS, ROWS, WIDE), BF),
            pltpu.VMEM((2, CHUNKS, ROWS, WIDE), BF),
            pltpu.VMEM((CHUNKS, ROWS, WIDE), BF),
            pltpu.VMEM((CHUNKS, ROWS, WIDE), BF),
            dma((6,)),
            dma((CHUNKS,)),
            dma((3,)),
            dma((5,)),
            dma((3,)),
            dma((12,)),
            dma((4, 4)),
            dma((4, 4)),
            dma((4, 4)),
            dma((2,)),
            dma((2,)),
            dma((2,)),
            dma((2, CHUNKS)),
            dma((2, CHUNKS)),
            dma((CHUNKS,)),
            dma((CHUNKS,)),
        ],
        compiler_params=pltpu.CompilerParams(
            collective_id=0, has_side_effects=True, vmem_limit_bytes=58 * 2**20
        ),
        name="block",
    )(noise_level, valid_len, span_mask, queries, keys, values, stream, latent, w_velocity.T, w_out)
    return pl.pallas_call(
        finish_kernel,
        out_shape=(
            jax.ShapeDtypeStruct((1, ROWS, MODEL), BF),
            jax.ShapeDtypeStruct((1, ROWS, 64), F32),
        ),
        in_specs=[anywhere] * 2,
        out_specs=(anywhere, anywhere),
        scratch_shapes=[
            pltpu.VMEM((1, ROWS, MODEL), BF),
            pltpu.VMEM((1, ROWS, 64), F32),
            dma((5,)),
            dma((5,)),
        ],
        compiler_params=pltpu.CompilerParams(vmem_limit_bytes=58 * 2**20),
        name="finish",
    )(rows, following)


def solution(mesh):
    rows = P("span", ("blk", "head"), None)
    return jax.shard_map(
        on_device,
        mesh=mesh,
        in_specs=(rows, rows, rows, rows, rows, P("head", None), P(), P(), P(), P()),
        out_specs=(rows, rows),
        check_vma=False,
    )
```

```python
import jax
import jax.numpy as jnp
from jax import lax
from jax.experimental import pallas as pl
from jax.experimental.pallas import tpu as pltpu
from jax.sharding import PartitionSpec as P

HD = 128
LEVELS = 8
SPANS = 4
BLKS = 16
ROWS = 24
HEADS = 32
SLOTS = 32
TOK = SLOTS * ROWS
MODEL = 6144
GROUP = 1024
CHUNKS = 6
WIDE = MODEL // CHUNKS
LOG_SCALE = HD ** -0.5 * 1.4426950408889634
TILE = 256
DEPTHS = (0, 1, 7, 2, 6, 3, 5, 4)
HOME = DEPTHS.index(0)
NEG = -1e30
MESH = pl.DeviceIdType.MESH
BF = jnp.bfloat16
F32 = jnp.float32


def place():
    span = lax.axis_index("span")
    blk = lax.axis_index("blk")
    head = lax.axis_index("head")
    return span, blk, lax.div(head, 2), lax.rem(head, 2)


def flip(blk):
    return blk + 1 - 2 * lax.rem(blk, 2)


def block_kernel(
    noise_ref, valid_ref, mask_ref, q_hbm, k_hbm, v_hbm, stream_hbm, latent_hbm, wv_hbm, w_hbm, out_ref, next_ref,
    q_in, k_in, v_in, stream_in, latent_in, wv_in, w_buf, q_got, kv_got, qx, kx, vx, acc, best, base, o_flat, o_buf,
    heads, lhs, near_out, near_in, far_out, far_in,
    in_sem, w_sem, a_send, a_recv, a_own, y_send, y_recv, c_send, c_recv, h_send, h_recv, h_own,
    n_send, n_recv, f_send, f_recv,
):
    span, blk, half, core = place()
    mine = half * BLKS + blk
    depth = lax.div(blk, 2)
    column = half * 2 + lax.rem(blk, 2)
    sibling = {"head": half * 2 + 1 - core}
    partner = {"blk": flip(blk), "head": (1 - half) * 2 + core}
    barrier = pltpu.get_barrier_semaphore()

    def greet(i, carry):
        other = lax.rem(mine + i, HEADS)
        pl.semaphore_signal(
            barrier, inc=1, device_id={"blk": lax.rem(other, BLKS), "head": lax.div(other, BLKS) * 2 + core},
            device_id_type=MESH,
        )
        return carry

    def greet_other(i, carry):
        pl.semaphore_signal(
            barrier, inc=1, device_id={"blk": lax.rem(blk + i, BLKS), "head": half * 2 + 1 - core}, device_id_type=MESH
        )
        return carry

    lax.fori_loop(1, HEADS, greet, 0)
    lax.fori_loop(0, BLKS, greet_other, 0)
    for i in range(1, SPANS):
        pl.semaphore_signal(barrier, inc=1, device_id={"span": lax.rem(span + i, SPANS)}, device_id_type=MESH)

    fetch = [
        pltpu.make_async_copy(src, dst, in_sem.at[i])
        for i, (src, dst) in enumerate(
            ((k_hbm, k_in), (v_hbm, v_in), (q_hbm, q_in), (stream_hbm, stream_in), (latent_hbm, latent_in), (wv_hbm, wv_in))
        )
    ]
    for copy in fetch:
        copy.start()
    loads = [
        pltpu.make_async_copy(w_hbm.at[:, pl.ds(n * WIDE, WIDE)], w_buf.at[n], w_sem.at[n]) for n in range(CHUNKS)
    ]
    lane = lax.broadcasted_iota(jnp.int32, (TOK, HD), 1)
    first = lane == 0
    row = lax.broadcasted_iota(jnp.int32, (TOK, HD), 0)
    turn = lax.div(row, ROWS)
    dz = jnp.zeros_like(turn)
    for step in range(8):
        dz = jnp.where(lax.div(turn, 4) == step, DEPTHS[step], dz)
    z = lax.rem(depth + 8 - dz, 8)
    x = lax.rem(column + 4 - lax.rem(turn, 4), 4)
    base[...] = (z * 2 + lax.rem(x, 2)) * (4 * ROWS) + lax.div(x, 2) * (2 * ROWS) + lax.rem(row, ROWS)
    unit = jnp.where(first, 1.0, 0.0).astype(BF)
    qx[:, HD:] = unit
    acc[...] = jnp.zeros_like(acc)
    best[...] = jnp.full_like(best, NEG)

    def prepare(c2, carry):
        limit = valid_ref[c2] * mask_ref[span, c2]
        for rel in range(2):
            here = pl.ds(rel * TOK, TOK)
            vx[c2, here, HD:] = unit
            pos = base[...] + lax.rem(core + rel, 2) * ROWS
            kx[c2, here, HD:] = jnp.where(first & (pos >= limit), NEG, 0.0).astype(BF)
        return carry

    lax.fori_loop(0, span + 1, prepare, 0)
    for i in range(3):
        fetch[i].wait()
    pl.semaphore_wait(barrier, HEADS - 1 + BLKS + SPANS - 1)

    def cols(head):
        return pl.ds(pl.multiple_of(head * HD, HD), HD)

    def target(dz, dx):
        z = lax.rem(depth + dz, 8)
        x = lax.rem(column + dx, 4)
        there = lax.div(x, 2)
        to = z * 2 + lax.rem(x, 2)
        return there * BLKS + to, {"blk": to, "head": there * 2 + core}, there

    own = [
        pltpu.make_async_copy(k_in.at[0, :, cols(mine)], kv_got.at[span, 0, HOME // 2, 0, HOME % 2 * 4], a_own.at[0]),
        pltpu.make_async_copy(v_in.at[0, :, cols(mine)], kv_got.at[span, 0, HOME // 2, 1, HOME % 2 * 4], a_own.at[1]),
        pltpu.make_async_copy(q_in.at[0, :, cols(mine)], q_got.at[BLKS + blk], a_own.at[2]),
    ]
    for step, dz in enumerate(DEPTHS):
        j, s = step // 2, step % 2 * 4

        def send_kv(dx, carry, dz=dz, j=j, s=s):
            other, device, there = target(dz, dx)
            for t, src in enumerate((k_in, v_in)):
                pltpu.make_async_remote_copy(
                    src.at[0, :, cols(other)], kv_got.at[span, 0, j, t, s + dx], a_send.at[t], a_recv.at[j],
                    device_id=device, device_id_type=MESH,
                ).start()
            return carry

        lax.fori_loop(0 if dz else 1, 4, send_kv, 0)
    for copy in own:
        copy.start()
    for dz in DEPTHS:

        def send_q(dx, carry, dz=dz):
            other, device, there = target(dz, dx)
            cross = lax.rem(half + there, 2)
            slot = (1 - cross) * BLKS + blk + cross * (1 - 2 * lax.rem(blk, 2))
            pltpu.make_async_remote_copy(
                q_in.at[0, :, cols(other)], q_got.at[slot], a_send.at[2], a_recv.at[4],
                device_id=device, device_id_type=MESH,
            ).start()
            return carry

        lax.fori_loop(0 if dz else 1, 4, send_q, 0)
    for load in loads:
        load.start()
    own[0].wait()
    own[1].wait()

    def arrived(j):
        count = 7 if j == HOME // 2 else 8
        whole = kv_got.at[0, 0, 0, :, pl.ds(0, count)]
        pltpu.make_async_copy(whole, whole, a_recv.at[j]).wait()

    def along(c2, j, to, which):
        return pltpu.make_async_remote_copy(
            kv_got.at[c2, 0, j], kv_got.at[c2, 0, j], y_send.at[which], y_recv.at[c2, j],
            device_id={"span": to}, device_id_type=MESH,
        )

    def beside(c2, j):
        return pltpu.make_async_remote_copy(
            kv_got.at[c2, 0, j], kv_got.at[c2, 1, j], c_send.at[c2, j], c_recv.at[c2, j],
            device_id=sibling, device_id_type=MESH,
        )

    plans = (
        "A0>3,1;A1>3,1;R11>3;A2>3,2,1;A3>3,2,1",
        "A0>2;A1>0,2;A2>3,2;A3>3,2",
        "A0>3;A1>3;R10>3;A2>3;A3>3",
        "A0;R00>2;A1;R01>2;A2;R20;R10;A3",
    )
    later = (("", ""), ("R00;R01;R02;R03", ""), ("R11;R12;R13;R00;R01", "R02;R03"), ("R21;R22;R23;R11", "R02;R03;R12;R13"))
    started = [([], []) for _ in range(SPANS)]

    def play(c, plan):
        sends, over = started[c]
        for event in plan.split(";") if plan else ():
            what, _, to = event.partition(">")
            if what[0] == "A":
                c2, j = c, int(what[1])
                arrived(j)
            else:
                c2, j = int(what[1]), int(what[2])
                along(c2, j, 0, 0).wait_recv()
            for t in to.split(",") if to else ():
                sends.append((c2, j, int(t), len(sends)))
                along(*sends[-1]).start()
            if c2 <= c:
                over.append((c2, j))
                beside(c2, j).start()

    def settle():
        for c in range(SPANS):

            @pl.when(span == c)
            def _(c=c):
                sends, over = started[c]
                for what in sends:
                    along(*what).wait_send()
                for what in over:
                    beside(*what).wait_send()


    for c in range(SPANS):

        @pl.when(span == c)
        def _(c=c):
            play(c, plans[c])

    own[2].wait()
    others = q_got.at[pl.ds(0, HEADS - 1)]
    pltpu.make_async_copy(others, others, a_recv.at[4]).wait()
    qx[:, :HD] = q_got[...].reshape(TOK, HD)

    goal = lax.div(blk, 8)
    rel = lax.rem(goal + core, 2)
    place_in = lax.rem(blk, 8)
    keep = goal == core

    def compute(c2, finish):
        for j in range(4):
            beside(c2, j).wait_recv()
        for r in range(2):
            here = pl.ds(r * TOK, TOK)
            kx[c2, here, :HD] = kv_got[c2, r, :, 0].reshape(TOK, HD)
            vx[c2, here, :HD] = kv_got[c2, r, :, 1].reshape(TOK, HD)
        for t in range(TOK // TILE):
            rows = slice(t * TILE, (t + 1) * TILE)
            scores = lax.dot_general(
                qx[rows], kx[c2], (((1,), (1,)), ((), ())), preferred_element_type=F32
            )
            old = best[rows]
            fresh = jnp.maximum(old, jnp.max(scores, axis=1, keepdims=True))
            unnorm = jnp.exp2(scores * LOG_SCALE - (fresh * LOG_SCALE)[:, :1]).astype(BF)
            part = jnp.dot(unnorm, vx[c2], preferred_element_type=F32)
            total = acc[rows] * jnp.exp2((old - fresh) * LOG_SCALE)[:, :1] + part
            if finish:
                o_flat[rows] = (total[:, :HD] / total[:, HD : HD + 1]).astype(BF)
                if t:
                    send_part(t - 1)
            else:
                acc[rows] = total
                best[rows] = fresh

    def send_part(part):
        here = pl.ds(part * BLKS, BLKS)
        o_buf[here] = o_flat[part * BLKS * ROWS : (part + 1) * BLKS * ROWS].reshape(BLKS, ROWS, HD)

        def send_o(other):
            pltpu.make_async_remote_copy(
                o_buf.at[part * BLKS + other], heads.at[part, rel, place_in], h_send.at[part], h_recv.at[part],
                device_id={"blk": other, "head": half * 2 + goal}, device_id_type=MESH,
            ).start()

        for dz in DEPTHS:
            for dx in range(2):
                if dz or dx:
                    send_o(lax.rem(depth + dz, 8) * 2 + lax.rem(blk + dx, 2))

        @pl.when(keep)
        def _():
            pltpu.make_async_copy(
                o_buf.at[part * BLKS + blk], heads.at[part, rel, place_in], h_own.at[part]
            ).start()

        @pl.when(jnp.logical_not(keep))
        def _():
            send_o(blk)

    def wait_part(part):
        most, every = o_buf.at[pl.ds(0, BLKS - 1)], o_buf.at[pl.ds(0, BLKS)]

        @pl.when(keep)
        def _():
            pltpu.make_async_copy(
                o_buf.at[part * BLKS + blk], heads.at[part, rel, place_in], h_own.at[part]
            ).wait()
            pltpu.make_async_copy(most, most, h_recv.at[part]).wait()
            pltpu.make_async_copy(most, most, h_send.at[part]).wait()

        @pl.when(jnp.logical_not(keep))
        def _():
            pltpu.make_async_copy(every, every, h_recv.at[part]).wait()
            pltpu.make_async_copy(every, every, h_send.at[part]).wait()

        for r in range(2):
            for j in range(8):
                lhs[part, r * ROWS : (r + 1) * ROWS, j * HD : (j + 1) * HD] = heads[part, r, j]

    def one_span(i, carry):
        compute(span - i, False)
        for c in range(1, SPANS):
            for turn, plan in enumerate(later[c]):
                if plan:

                    @pl.when((span == c) & (i == turn))
                    def _(c=c, plan=plan):
                        play(c, plan)

        return carry

    lax.fori_loop(0, span, one_span, 0)
    compute(0, True)

    def near(part, n):
        return pltpu.make_async_remote_copy(
            near_out.at[part, n], near_in.at[part, n], n_send.at[part, n], n_recv.at[part, n],
            device_id=sibling, device_id_type=MESH,
        )

    def far(n):
        return pltpu.make_async_remote_copy(
            far_out.at[n], far_in.at[n], f_send.at[n], f_recv.at[n], device_id=partner, device_id_type=MESH
        )

    wait_part(0)
    held = [None] * CHUNKS
    for n in range(CHUNKS + 1):
        if n < CHUNKS:
            loads[n].wait()
            part = jnp.dot(lhs[0], w_buf[n], preferred_element_type=F32)
            near_out[0, n] = part[ROWS:].astype(BF)
            near(0, n).start()
            held[n] = part[:ROWS]
        m = n - 1
        if 0 <= m < CHUNKS:
            near(0, m).wait_recv()
            far_out[m] = (held[m] + near_in[0, m].astype(F32)).astype(BF)
            far(m).start()
    wait_part(1)
    for n in range(CHUNKS):
        part = jnp.dot(lhs[1], w_buf[n], preferred_element_type=F32)
        near_out[1, n] = part[ROWS:].astype(BF)
        near(1, n).start()
        held[n] = part[:ROWS]
    for i in range(3, 6):
        fetch[i].wait()
    velocity = jnp.zeros((ROWS, 64), F32)
    for m in range(CHUNKS):
        near(1, m).wait_recv()
        far(m).wait_recv()
        here = slice(m * WIDE, (m + 1) * WIDE)
        update = held[m] + near_in[1, m].astype(F32) + far_in[m].astype(F32)
        fresh = (stream_in[0, :, here].astype(F32) + update).astype(BF)
        out_ref[0, :, here] = fresh
        velocity += lax.dot_general(
            fresh, wv_in[:, here], (((1,), (1,)), ((), ())), preferred_element_type=F32
        )
    level = jnp.full((ROWS, 64), noise_ref[span], jnp.int32).astype(F32)

    def sigma(value):
        u = 1.0 - value / LEVELS
        return 3.0 * u / (1.0 + 2.0 * u)

    next_ref[0] = latent_in[0] + (sigma(level + 1.0) - sigma(level)) * velocity
    settle()
    for t in range(3):
        pltpu.make_async_copy(others, others, a_send.at[t]).wait()
    for n in range(CHUNKS):
        near(0, n).wait_send()
        near(1, n).wait_send()
        far(n).wait_send()


def finish_kernel(rows_in, next_in, rows_out, next_out, rows_buf, next_buf, in_sem, out_sem):
    wide = MODEL // 4
    first, second = [], []
    for n in range(4):
        here = (slice(None), slice(None), pl.ds(n * wide, wide))
        first.append(pltpu.make_async_copy(rows_in.at[here], rows_buf.at[here], in_sem.at[n]))
        second.append(pltpu.make_async_copy(rows_buf.at[here], rows_out.at[here], out_sem.at[n]))
    first.append(pltpu.make_async_copy(next_in, next_buf, in_sem.at[4]))
    second.append(pltpu.make_async_copy(next_buf, next_out, out_sem.at[4]))
    for copy in first:
        copy.start()
    for one, two in zip(first, second):
        one.wait()
        two.start()
    for copy in second:
        copy.wait()


def on_device(
    queries, keys, values, stream, latent, w_out, w_velocity, noise_level, valid_len, span_mask
):
    anywhere = pl.BlockSpec(memory_space=pl.ANY)
    sm = pl.BlockSpec(memory_space=pltpu.SMEM)
    vm = pl.BlockSpec(memory_space=pltpu.VMEM)
    dma = pltpu.SemaphoreType.DMA
    rows, following = pl.pallas_call(
        block_kernel,
        out_shape=(
            jax.ShapeDtypeStruct((1, ROWS, MODEL), BF),
            jax.ShapeDtypeStruct((1, ROWS, 64), F32),
        ),
        in_specs=[sm] * 3 + [anywhere] * 7,
        out_specs=(vm, vm),
        scratch_shapes=[
            pltpu.VMEM((1, ROWS, HEADS * HD), BF),
            pltpu.VMEM((1, ROWS, HEADS * HD), BF),
            pltpu.VMEM((1, ROWS, HEADS * HD), BF),
            pltpu.VMEM((1, ROWS, MODEL), BF),
            pltpu.VMEM((1, ROWS, 64), F32),
            pltpu.VMEM((64, MODEL), BF),
            pltpu.VMEM((CHUNKS, GROUP, WIDE), BF),
            pltpu.VMEM((SLOTS, ROWS, HD), BF),
            pltpu.VMEM((SPANS, 2, 4, 2, 8, ROWS, HD), BF),
            pltpu.VMEM((TOK, 2 * HD), BF),
            pltpu.VMEM((SPANS, 2 * TOK, 2 * HD), BF),
            pltpu.VMEM((SPANS, 2 * TOK, 2 * HD), BF),
            pltpu.VMEM((TOK, 2 * HD), F32),
            pltpu.VMEM((TOK, HD), F32),
            pltpu.VMEM((TOK, HD), jnp.int32),
            pltpu.VMEM((TOK, HD), BF),
            pltpu.VMEM((SLOTS, ROWS, HD), BF),
            pltpu.VMEM((2, 2, 8, ROWS, HD), BF),
            pltpu.VMEM((2, 2 * ROWS, GROUP), BF),
            pltpu.VMEM((2, CHUNKS, ROWS, WIDE), BF),
            pltpu.VMEM((2, CHUNKS, ROWS, WIDE), BF),
            pltpu.VMEM((CHUNKS, ROWS, WIDE), BF),
            pltpu.VMEM((CHUNKS, ROWS, WIDE), BF),
            dma((6,)),
            dma((CHUNKS,)),
            dma((3,)),
            dma((5,)),
            dma((3,)),
            dma((12,)),
            dma((4, 4)),
            dma((4, 4)),
            dma((4, 4)),
            dma((2,)),
            dma((2,)),
            dma((2,)),
            dma((2, CHUNKS)),
            dma((2, CHUNKS)),
            dma((CHUNKS,)),
            dma((CHUNKS,)),
        ],
        compiler_params=pltpu.CompilerParams(
            collective_id=0, has_side_effects=True, vmem_limit_bytes=58 * 2**20
        ),
        name="block",
    )(noise_level, valid_len, span_mask, queries, keys, values, stream, latent, w_velocity.T, w_out)
    return pl.pallas_call(
        finish_kernel,
        out_shape=(
            jax.ShapeDtypeStruct((1, ROWS, MODEL), BF),
            jax.ShapeDtypeStruct((1, ROWS, 64), F32),
        ),
        in_specs=[anywhere] * 2,
        out_specs=(anywhere, anywhere),
        scratch_shapes=[
            pltpu.VMEM((1, ROWS, MODEL), BF),
            pltpu.VMEM((1, ROWS, 64), F32),
            dma((5,)),
            dma((5,)),
        ],
        compiler_params=pltpu.CompilerParams(vmem_limit_bytes=58 * 2**20),
        name="finish",
    )(rows, following)


def solution(mesh):
    rows = P("span", ("blk", "head"), None)
    return jax.shard_map(
        on_device,
        mesh=mesh,
        in_specs=(rows, rows, rows, rows, rows, P("head", None), P(), P(), P(), P()),
        out_specs=(rows, rows),
        check_vma=False,
    )
```

```python
import jax
import jax.numpy as jnp
from jax import lax
from jax.experimental import pallas as pl
from jax.experimental.pallas import tpu as pltpu
from jax.sharding import PartitionSpec as P

HD = 128
LEVELS = 8
SPANS = 4
BLKS = 16
ROWS = 24
HEADS = 32
SLOTS = 32
TOK = SLOTS * ROWS
MODEL = 6144
GROUP = 1024
CHUNKS = 6
WIDE = MODEL // CHUNKS
LOG_SCALE = HD ** -0.5 * 1.4426950408889634
TILE = 256
DEPTHS = (0, 1, 7, 2, 6, 3, 5, 4)
HOME = DEPTHS.index(0)
NEG = -1e30
MESH = pl.DeviceIdType.MESH
BF = jnp.bfloat16
F32 = jnp.float32


def place():
    span = lax.axis_index("span")
    blk = lax.axis_index("blk")
    head = lax.axis_index("head")
    return span, blk, lax.div(head, 2), lax.rem(head, 2)


def flip(blk):
    return blk + 1 - 2 * lax.rem(blk, 2)


def block_kernel(
    noise_ref, valid_ref, mask_ref, q_hbm, k_hbm, v_hbm, stream_hbm, latent_hbm, wv_hbm, w_hbm, out_ref, next_ref,
    q_in, k_in, v_in, stream_in, latent_in, wv_in, w_buf, q_got, kv_got, qx, kx, vx, acc, best, base, o_flat, o_buf,
    heads, lhs, near_out, near_in, far_out, far_in,
    in_sem, w_sem, a_send, a_recv, a_own, y_send, y_recv, c_send, c_recv, h_send, h_recv, h_own,
    n_send, n_recv, f_send, f_recv,
):
    span, blk, half, core = place()
    mine = half * BLKS + blk
    depth = lax.div(blk, 2)
    column = half * 2 + lax.rem(blk, 2)
    sibling = {"head": half * 2 + 1 - core}
    partner = {"blk": flip(blk), "head": (1 - half) * 2 + core}
    barrier = pltpu.get_barrier_semaphore()

    def greet(i, carry):
        other = lax.rem(mine + i, HEADS)
        pl.semaphore_signal(
            barrier, inc=1, device_id={"blk": lax.rem(other, BLKS), "head": lax.div(other, BLKS) * 2 + core},
            device_id_type=MESH,
        )
        return carry

    def greet_other(i, carry):
        pl.semaphore_signal(
            barrier, inc=1, device_id={"blk": lax.rem(blk + i, BLKS), "head": half * 2 + 1 - core}, device_id_type=MESH
        )
        return carry

    lax.fori_loop(1, HEADS, greet, 0)
    lax.fori_loop(0, BLKS, greet_other, 0)
    for i in range(1, SPANS):
        pl.semaphore_signal(barrier, inc=1, device_id={"span": lax.rem(span + i, SPANS)}, device_id_type=MESH)

    fetch = [
        pltpu.make_async_copy(src, dst, in_sem.at[i])
        for i, (src, dst) in enumerate(
            ((k_hbm, k_in), (v_hbm, v_in), (q_hbm, q_in), (stream_hbm, stream_in), (latent_hbm, latent_in), (wv_hbm, wv_in))
        )
    ]
    for copy in fetch:
        copy.start()
    loads = [
        pltpu.make_async_copy(w_hbm.at[:, pl.ds(n * WIDE, WIDE)], w_buf.at[n], w_sem.at[n]) for n in range(CHUNKS)
    ]
    lane = lax.broadcasted_iota(jnp.int32, (TOK, HD), 1)
    first = lane == 0
    row = lax.broadcasted_iota(jnp.int32, (TOK, HD), 0)
    turn = lax.div(row, ROWS)
    dz = jnp.zeros_like(turn)
    for step in range(8):
        dz = jnp.where(lax.div(turn, 4) == step, DEPTHS[step], dz)
    z = lax.rem(depth + 8 - dz, 8)
    x = lax.rem(column + 4 - lax.rem(turn, 4), 4)
    base[...] = (z * 2 + lax.rem(x, 2)) * (4 * ROWS) + lax.div(x, 2) * (2 * ROWS) + lax.rem(row, ROWS)
    unit = jnp.where(first, 1.0, 0.0).astype(BF)
    qx[:, HD:] = unit
    acc[...] = jnp.zeros_like(acc)
    best[...] = jnp.full_like(best, NEG)

    def prepare(c2, carry):
        limit = valid_ref[c2] * mask_ref[span, c2]
        for rel in range(2):
            here = pl.ds(rel * TOK, TOK)
            vx[c2, here, HD:] = unit
            pos = base[...] + lax.rem(core + rel, 2) * ROWS
            kx[c2, here, HD:] = jnp.where(first & (pos >= limit), NEG, 0.0).astype(BF)
        return carry

    lax.fori_loop(0, span + 1, prepare, 0)
    for i in range(3):
        fetch[i].wait()
    pl.semaphore_wait(barrier, HEADS - 1 + BLKS + SPANS - 1)

    def cols(head):
        return pl.ds(pl.multiple_of(head * HD, HD), HD)

    def target(dz, dx):
        z = lax.rem(depth + dz, 8)
        x = lax.rem(column + dx, 4)
        there = lax.div(x, 2)
        to = z * 2 + lax.rem(x, 2)
        return there * BLKS + to, {"blk": to, "head": there * 2 + core}, there

    own = [
        pltpu.make_async_copy(k_in.at[0, :, cols(mine)], kv_got.at[span, 0, HOME // 2, 0, HOME % 2 * 4], a_own.at[0]),
        pltpu.make_async_copy(v_in.at[0, :, cols(mine)], kv_got.at[span, 0, HOME // 2, 1, HOME % 2 * 4], a_own.at[1]),
        pltpu.make_async_copy(q_in.at[0, :, cols(mine)], q_got.at[BLKS + blk], a_own.at[2]),
    ]
    for step, dz in enumerate(DEPTHS):
        j, s = step // 2, step % 2 * 4

        def send_kv(dx, carry, dz=dz, j=j, s=s):
            other, device, there = target(dz, dx)
            for t, src in enumerate((k_in, v_in)):
                pltpu.make_async_remote_copy(
                    src.at[0, :, cols(other)], kv_got.at[span, 0, j, t, s + dx], a_send.at[t], a_recv.at[j],
                    device_id=device, device_id_type=MESH,
                ).start()
            return carry

        lax.fori_loop(0 if dz else 1, 4, send_kv, 0)
    for copy in own:
        copy.start()
    for dz in DEPTHS:

        def send_q(dx, carry, dz=dz):
            other, device, there = target(dz, dx)
            cross = lax.rem(half + there, 2)
            slot = (1 - cross) * BLKS + blk + cross * (1 - 2 * lax.rem(blk, 2))
            pltpu.make_async_remote_copy(
                q_in.at[0, :, cols(other)], q_got.at[slot], a_send.at[2], a_recv.at[4],
                device_id=device, device_id_type=MESH,
            ).start()
            return carry

        lax.fori_loop(0 if dz else 1, 4, send_q, 0)
    for load in loads:
        load.start()
    own[0].wait()
    own[1].wait()

    def arrived(j):
        count = 7 if j == HOME // 2 else 8
        whole = kv_got.at[0, 0, 0, :, pl.ds(0, count)]
        pltpu.make_async_copy(whole, whole, a_recv.at[j]).wait()

    def along(c2, j, to, which):
        return pltpu.make_async_remote_copy(
            kv_got.at[c2, 0, j], kv_got.at[c2, 0, j], y_send.at[which], y_recv.at[c2, j],
            device_id={"span": to}, device_id_type=MESH,
        )

    def beside(c2, j):
        return pltpu.make_async_remote_copy(
            kv_got.at[c2, 0, j], kv_got.at[c2, 1, j], c_send.at[c2, j], c_recv.at[c2, j],
            device_id=sibling, device_id_type=MESH,
        )

    plans = (
        "A0>3,1;A1>3,1;R11>3;A2>3,2,1;A3>3,2,1",
        "A0>2;A1>0,2;A2>3,2;A3>3,2",
        "A0>3;A1>3;R10>3;A2>3;A3>3",
        "A0;R00>2;A1;R01>2;A2;R20;R10;A3",
    )
    later = (("", ""), ("R00;R01;R02;R03", ""), ("R11;R12;R13;R00;R01", "R02;R03"), ("R21;R22;R23;R11", "R02;R03;R12;R13"))
    started = [([], []) for _ in range(SPANS)]

    def play(c, plan):
        sends, over = started[c]
        for event in plan.split(";") if plan else ():
            what, _, to = event.partition(">")
            if what[0] == "A":
                c2, j = c, int(what[1])
                arrived(j)
            else:
                c2, j = int(what[1]), int(what[2])
                along(c2, j, 0, 0).wait_recv()
            for t in to.split(",") if to else ():
                sends.append((c2, j, int(t), len(sends)))
                along(*sends[-1]).start()
            if c2 <= c:
                over.append((c2, j))
                beside(c2, j).start()

    def settle():
        for c in range(SPANS):

            @pl.when(span == c)
            def _(c=c):
                sends, over = started[c]
                for what in sends:
                    along(*what).wait_send()
                for what in over:
                    beside(*what).wait_send()


    for c in range(SPANS):

        @pl.when(span == c)
        def _(c=c):
            play(c, plans[c])

    def pack(c2):
        for r in range(2):
            if r:
                for j in range(4):
                    beside(c2, j).wait_recv()
            here = pl.ds(r * TOK, TOK)
            kx[c2, here, :HD] = kv_got[c2, r, :, 0].reshape(TOK, HD)
            vx[c2, here, :HD] = kv_got[c2, r, :, 1].reshape(TOK, HD)

    pack(span)
    own[2].wait()
    others = q_got.at[pl.ds(0, HEADS - 1)]
    pltpu.make_async_copy(others, others, a_recv.at[4]).wait()
    qx[:, :HD] = q_got[...].reshape(TOK, HD)

    goal = lax.div(blk, 8)
    rel = lax.rem(goal + core, 2)
    place_in = lax.rem(blk, 8)
    keep = goal == core

    def compute(c2, finish):
        for t in range(TOK // TILE):
            rows = slice(t * TILE, (t + 1) * TILE)
            scores = lax.dot_general(
                qx[rows], kx[c2], (((1,), (1,)), ((), ())), preferred_element_type=F32
            )
            old = best[rows]
            fresh = jnp.maximum(old, jnp.max(scores, axis=1, keepdims=True))
            unnorm = jnp.exp2(scores * LOG_SCALE - (fresh * LOG_SCALE)[:, :1]).astype(BF)
            part = jnp.dot(unnorm, vx[c2], preferred_element_type=F32)
            total = acc[rows] * jnp.exp2((old - fresh) * LOG_SCALE)[:, :1] + part
            if finish:
                o_flat[rows] = (total[:, :HD] / total[:, HD : HD + 1]).astype(BF)
                if t:
                    send_part(t - 1)
            else:
                acc[rows] = total
                best[rows] = fresh

    def send_part(part):
        here = pl.ds(part * BLKS, BLKS)
        o_buf[here] = o_flat[part * BLKS * ROWS : (part + 1) * BLKS * ROWS].reshape(BLKS, ROWS, HD)

        def send_o(other):
            pltpu.make_async_remote_copy(
                o_buf.at[part * BLKS + other], heads.at[part, rel, place_in], h_send.at[part], h_recv.at[part],
                device_id={"blk": other, "head": half * 2 + goal}, device_id_type=MESH,
            ).start()

        for dz in DEPTHS:
            for dx in range(2):
                if dz or dx:
                    send_o(lax.rem(depth + dz, 8) * 2 + lax.rem(blk + dx, 2))

        @pl.when(keep)
        def _():
            pltpu.make_async_copy(
                o_buf.at[part * BLKS + blk], heads.at[part, rel, place_in], h_own.at[part]
            ).start()

        @pl.when(jnp.logical_not(keep))
        def _():
            send_o(blk)

    def wait_part(part):
        most, every = o_buf.at[pl.ds(0, BLKS - 1)], o_buf.at[pl.ds(0, BLKS)]

        @pl.when(keep)
        def _():
            pltpu.make_async_copy(
                o_buf.at[part * BLKS + blk], heads.at[part, rel, place_in], h_own.at[part]
            ).wait()
            pltpu.make_async_copy(most, most, h_recv.at[part]).wait()
            pltpu.make_async_copy(most, most, h_send.at[part]).wait()

        @pl.when(jnp.logical_not(keep))
        def _():
            pltpu.make_async_copy(every, every, h_recv.at[part]).wait()
            pltpu.make_async_copy(every, every, h_send.at[part]).wait()

        for r in range(2):
            for j in range(8):
                lhs[part, r * ROWS : (r + 1) * ROWS, j * HD : (j + 1) * HD] = heads[part, r, j]

    def one_span(i, carry):
        compute(span - i, False)
        for c in range(1, SPANS):
            for turn, plan in enumerate(later[c]):
                if plan:

                    @pl.when((span == c) & (i == turn))
                    def _(c=c, plan=plan):
                        play(c, plan)

        pack(span - i - 1)
        return carry

    lax.fori_loop(0, span, one_span, 0)
    compute(0, True)

    def near(part, n):
        return pltpu.make_async_remote_copy(
            near_out.at[part, n], near_in.at[part, n], n_send.at[part, n], n_recv.at[part, n],
            device_id=sibling, device_id_type=MESH,
        )

    def far(n):
        return pltpu.make_async_remote_copy(
            far_out.at[n], far_in.at[n], f_send.at[n], f_recv.at[n], device_id=partner, device_id_type=MESH
        )

    wait_part(0)
    held = [None] * CHUNKS
    for n in range(CHUNKS + 1):
        if n < CHUNKS:
            loads[n].wait()
            part = jnp.dot(lhs[0], w_buf[n], preferred_element_type=F32)
            near_out[0, n] = part[ROWS:].astype(BF)
            near(0, n).start()
            held[n] = part[:ROWS]
        m = n - 1
        if 0 <= m < CHUNKS:
            near(0, m).wait_recv()
            far_out[m] = (held[m] + near_in[0, m].astype(F32)).astype(BF)
            far(m).start()
    wait_part(1)
    for n in range(CHUNKS):
        part = jnp.dot(lhs[1], w_buf[n], preferred_element_type=F32)
        near_out[1, n] = part[ROWS:].astype(BF)
        near(1, n).start()
        held[n] = part[:ROWS]
    for i in range(3, 6):
        fetch[i].wait()
    velocity = jnp.zeros((ROWS, 64), F32)
    for m in range(CHUNKS):
        near(1, m).wait_recv()
        far(m).wait_recv()
        here = slice(m * WIDE, (m + 1) * WIDE)
        update = held[m] + near_in[1, m].astype(F32) + far_in[m].astype(F32)
        fresh = (stream_in[0, :, here].astype(F32) + update).astype(BF)
        out_ref[0, :, here] = fresh
        velocity += lax.dot_general(
            fresh, wv_in[:, here], (((1,), (1,)), ((), ())), preferred_element_type=F32
        )
    level = jnp.full((ROWS, 64), noise_ref[span], jnp.int32).astype(F32)

    def sigma(value):
        u = 1.0 - value / LEVELS
        return 3.0 * u / (1.0 + 2.0 * u)

    next_ref[0] = latent_in[0] + (sigma(level + 1.0) - sigma(level)) * velocity
    settle()
    for t in range(3):
        pltpu.make_async_copy(others, others, a_send.at[t]).wait()
    for n in range(CHUNKS):
        near(0, n).wait_send()
        near(1, n).wait_send()
        far(n).wait_send()


def finish_kernel(rows_in, next_in, rows_out, next_out, rows_buf, next_buf, in_sem, out_sem):
    wide = MODEL // 4
    first, second = [], []
    for n in range(4):
        here = (slice(None), slice(None), pl.ds(n * wide, wide))
        first.append(pltpu.make_async_copy(rows_in.at[here], rows_buf.at[here], in_sem.at[n]))
        second.append(pltpu.make_async_copy(rows_buf.at[here], rows_out.at[here], out_sem.at[n]))
    first.append(pltpu.make_async_copy(next_in, next_buf, in_sem.at[4]))
    second.append(pltpu.make_async_copy(next_buf, next_out, out_sem.at[4]))
    for copy in first:
        copy.start()
    for one, two in zip(first, second):
        one.wait()
        two.start()
    for copy in second:
        copy.wait()


def on_device(
    queries, keys, values, stream, latent, w_out, w_velocity, noise_level, valid_len, span_mask
):
    anywhere = pl.BlockSpec(memory_space=pl.ANY)
    sm = pl.BlockSpec(memory_space=pltpu.SMEM)
    vm = pl.BlockSpec(memory_space=pltpu.VMEM)
    dma = pltpu.SemaphoreType.DMA
    rows, following = pl.pallas_call(
        block_kernel,
        out_shape=(
            jax.ShapeDtypeStruct((1, ROWS, MODEL), BF),
            jax.ShapeDtypeStruct((1, ROWS, 64), F32),
        ),
        in_specs=[sm] * 3 + [anywhere] * 7,
        out_specs=(vm, vm),
        scratch_shapes=[
            pltpu.VMEM((1, ROWS, HEADS * HD), BF),
            pltpu.VMEM((1, ROWS, HEADS * HD), BF),
            pltpu.VMEM((1, ROWS, HEADS * HD), BF),
            pltpu.VMEM((1, ROWS, MODEL), BF),
            pltpu.VMEM((1, ROWS, 64), F32),
            pltpu.VMEM((64, MODEL), BF),
            pltpu.VMEM((CHUNKS, GROUP, WIDE), BF),
            pltpu.VMEM((SLOTS, ROWS, HD), BF),
            pltpu.VMEM((SPANS, 2, 4, 2, 8, ROWS, HD), BF),
            pltpu.VMEM((TOK, 2 * HD), BF),
            pltpu.VMEM((SPANS, 2 * TOK, 2 * HD), BF),
            pltpu.VMEM((SPANS, 2 * TOK, 2 * HD), BF),
            pltpu.VMEM((TOK, 2 * HD), F32),
            pltpu.VMEM((TOK, HD), F32),
            pltpu.VMEM((TOK, HD), jnp.int32),
            pltpu.VMEM((TOK, HD), BF),
            pltpu.VMEM((SLOTS, ROWS, HD), BF),
            pltpu.VMEM((2, 2, 8, ROWS, HD), BF),
            pltpu.VMEM((2, 2 * ROWS, GROUP), BF),
            pltpu.VMEM((2, CHUNKS, ROWS, WIDE), BF),
            pltpu.VMEM((2, CHUNKS, ROWS, WIDE), BF),
            pltpu.VMEM((CHUNKS, ROWS, WIDE), BF),
            pltpu.VMEM((CHUNKS, ROWS, WIDE), BF),
            dma((6,)),
            dma((CHUNKS,)),
            dma((3,)),
            dma((5,)),
            dma((3,)),
            dma((12,)),
            dma((4, 4)),
            dma((4, 4)),
            dma((4, 4)),
            dma((2,)),
            dma((2,)),
            dma((2,)),
            dma((2, CHUNKS)),
            dma((2, CHUNKS)),
            dma((CHUNKS,)),
            dma((CHUNKS,)),
        ],
        compiler_params=pltpu.CompilerParams(
            collective_id=0, has_side_effects=True, vmem_limit_bytes=58 * 2**20
        ),
        name="block",
    )(noise_level, valid_len, span_mask, queries, keys, values, stream, latent, w_velocity.T, w_out)
    return pl.pallas_call(
        finish_kernel,
        out_shape=(
            jax.ShapeDtypeStruct((1, ROWS, MODEL), BF),
            jax.ShapeDtypeStruct((1, ROWS, 64), F32),
        ),
        in_specs=[anywhere] * 2,
        out_specs=(anywhere, anywhere),
        scratch_shapes=[
            pltpu.VMEM((1, ROWS, MODEL), BF),
            pltpu.VMEM((1, ROWS, 64), F32),
            dma((5,)),
            dma((5,)),
        ],
        compiler_params=pltpu.CompilerParams(vmem_limit_bytes=58 * 2**20),
        name="finish",
    )(rows, following)


def solution(mesh):
    rows = P("span", ("blk", "head"), None)
    return jax.shard_map(
        on_device,
        mesh=mesh,
        in_specs=(rows, rows, rows, rows, rows, P("head", None), P(), P(), P(), P()),
        out_specs=(rows, rows),
        check_vma=False,
    )
```
